256 devices in a mesh: lo: 16 (over z_hi, x, core), hi: 16 (over z_lo, y).
Axes of the slice: x: 4, y: 4, z: 8 (z_hi: 2, z_lo: 4; z = z_hi * 4 + z_lo), core: 2. Of those that a mesh axis runs over, the one named last changes fastest.
Arguments:
- queries: bfloat16 [65536, 512], P(('hi', 'lo')), may hold values from -20 to 20
- keys: bfloat16 [65536, 512], P(('hi', 'lo')), may hold values from -20 to 20
- values: bfloat16 [65536, 512], P(('hi', 'lo')), may hold values from -20 to 20
- cotangent: bfloat16 [65536, 512], P(('hi', 'lo')), may hold values from -6 to 6
Outputs:
- mixed: bfloat16 [65536, 512], P(('hi', 'lo'))
- grad_queries: bfloat16 [65536, 512], P(('hi', 'lo'))
- grad_keys: bfloat16 [65536, 512], P(('hi', 'lo'))
- grad_values: bfloat16 [65536, 512], P(('hi', 'lo'))
The draws below stay inside these ranges and needn't reach their ends.
All inputs are finite; a program needn't handle non-finite values.
Results may differ from the reference program's by a relative error of at most 0.007.
Values may be sent and summed in bfloat16 or wider, within the bound.
No kernel may reach another device: no remote copies, remote signals or barrier semaphores. Data moves between devices by JAX's collectives and lax.ppermute only.
A program may use at most 64 MiB of HBM per device.

```python
import jax
import jax.numpy as jnp
from jax import lax

D = 512
HEAD_DIM = 64
HEADS = 8
TOK_DEV = 256
COARSE = 64
LEVELS = 8
TOKENS = 65536
N_LO = 16
N_HI = 16


def multiscale(key):
    blocks = TOKENS // TOK_DEV
    block_of = jnp.arange(TOKENS) // TOK_DEV
    total = jnp.zeros((TOKENS, D), jnp.float32)
    for section in range(LEVELS + 1):
        count = max(blocks >> section, 1)
        table = jax.random.normal(jax.random.fold_in(key, section), (count, D), jnp.float32)
        total = total + 0.35 * table[jnp.minimum(block_of >> section, count - 1)]
    return total


def draw_queries(key, part):
    key = jax.random.fold_in(key, 12)
    result = jnp.clip(jax.random.normal(key, (TOKENS, D), jnp.float32), -4.0, 4.0)
    return jnp.clip(result, -20.0, 20.0).astype(jnp.bfloat16)


def draw_keys(key, part):
    key = jax.random.fold_in(key, 11)
    offsets = multiscale(jax.random.fold_in(key, 1))
    rough = jnp.clip(jax.random.normal(key, (TOKENS, D), jnp.float32), -4.0, 4.0)
    result = rough + offsets
    return jnp.clip(result, -20.0, 20.0).astype(jnp.bfloat16)


def draw_values(key, part):
    key = jax.random.fold_in(key, 13)
    offsets = multiscale(jax.random.fold_in(key, 1))
    rough = jnp.clip(jax.random.normal(key, (TOKENS, D), jnp.float32), -4.0, 4.0)
    return jnp.clip(rough + offsets, -20.0, 20.0).astype(jnp.bfloat16)


def block_scale(rng, shape, cuts, smallest, high):
    factor_of, own = 1.0, jax.random.fold_in(rng, 6)
    for dim, shards_of in cuts:
        steps = jnp.exp(jax.random.uniform(jax.random.fold_in(own, dim), (shards_of,), jnp.float32, smallest / len(cuts), high / len(cuts)))
        factor_of = factor_of * jnp.repeat(steps, shape[dim] // shards_of).reshape([-1 if axis == dim else 1 for axis in range(len(shape))])
    return factor_of


def bell_draw(key, dims, deviation, most, cuts=(), kind=jnp.bfloat16):
    factor_of = block_scale(key, dims, cuts, -0.22, 0.18) if cuts else 1.0
    array = jax.random.normal(key, dims, jnp.float32) * deviation * factor_of
    return jnp.minimum(jnp.maximum(array, -most), most).astype(kind)


def setup_inputs(seed: int = 0) -> dict:
    seeds = jax.random.split(jax.random.key(seed), 5)
    return {
        "queries": draw_queries(jax.random.fold_in(seeds[4], 71), 0),
        "keys": draw_keys(jax.random.fold_in(seeds[4], 71), 0),
        "values": draw_values(jax.random.fold_in(seeds[4], 71), 0),
        "cotangent": bell_draw(seeds[3], (TOKENS, D), 1.0, 6.0, ((0, 256),)),
    }


def to_bfloat(numbers):
    return lax.optimization_barrier(numbers.astype(jnp.bfloat16)).astype(jnp.float32)


def pool_groups(groups):
    count = groups.shape[0] // 2
    joined = jnp.concatenate([groups[0::2], groups[1::2]], axis=1)
    return to_bfloat(joined.reshape(count, COARSE, 2, groups.shape[2]).mean(axis=2))


def spread_groups(gradient):
    count, rows, width = gradient.shape
    doubled = jnp.broadcast_to(0.5 * gradient[:, :, None, :], (count, rows, 2, width)).reshape(count, 2 * rows, width)
    return jnp.stack([doubled[:, :rows], doubled[:, rows:]], axis=1).reshape(2 * count, rows, width)


def attend(query_rows, key_rows, value_rows, grad_rows):
    scale = HEAD_DIM ** -0.5
    high = lax.Precision.HIGHEST
    query_heads = query_rows.reshape(query_rows.shape[0], HEADS, HEAD_DIM)
    key_heads = key_rows.reshape(key_rows.shape[0], HEADS, HEAD_DIM)
    value_heads = value_rows.reshape(value_rows.shape[0], HEADS, HEAD_DIM)
    grad_heads = grad_rows.reshape(grad_rows.shape[0], HEADS, HEAD_DIM)
    scores = jnp.einsum("che,khe->hck", query_heads, key_heads, precision=high) * scale
    largest = jnp.max(scores, axis=-1, keepdims=True)
    expsc = jnp.exp(scores - largest)
    probs = expsc / jnp.sum(expsc, axis=-1, keepdims=True)
    weights = to_bfloat(probs)
    mixed = jnp.einsum("hck,khe->che", weights, value_heads, precision=high)
    dprobs = jnp.einsum("che,khe->hck", grad_heads, value_heads, precision=high)
    inner = jnp.sum(probs * dprobs, axis=-1, keepdims=True)
    dscores = to_bfloat(probs * (dprobs - inner))
    grad_query = jnp.einsum("hck,khe->che", dscores, key_heads, precision=high) * scale
    grad_key = jnp.einsum("hck,che->khe", dscores, query_heads, precision=high) * scale
    grad_value = jnp.einsum("hck,che->khe", weights, grad_heads, precision=high)
    rows_here = query_rows.shape[0]
    keys_here = key_rows.shape[0]
    return (mixed.reshape(rows_here, D), grad_query.reshape(rows_here, D),
            grad_key.reshape(keys_here, D), grad_value.reshape(keys_here, D))


def reference(queries, keys, values, cotangent):
    blocks = N_LO * N_HI
    pool_factor = TOK_DEV // COARSE
    query_blocks = queries.reshape(blocks, TOK_DEV, D)
    key_blocks = keys.reshape(blocks, TOK_DEV, D)
    value_blocks = values.reshape(blocks, TOK_DEV, D)
    grad_blocks = cotangent.reshape(blocks, TOK_DEV, D)

    def first_level(source):
        return to_bfloat(source.astype(jnp.float32).reshape(blocks, COARSE, pool_factor, D).mean(axis=2))

    key_levels = [first_level(keys)]
    value_levels = [first_level(values)]
    for section in range(1, LEVELS):
        key_levels.append(pool_groups(key_levels[-1]))
        value_levels.append(pool_groups(value_levels[-1]))

    def visit(carry, block_index):
        key_grads, value_grads = carry
        siblings = [jnp.bitwise_xor(jnp.right_shift(block_index, section), 1).astype(jnp.int32) for section in range(LEVELS)]
        query_rows = lax.dynamic_index_in_dim(query_blocks, block_index, 0, keepdims=False).astype(jnp.float32)
        key_rows = lax.dynamic_index_in_dim(key_blocks, block_index, 0, keepdims=False).astype(jnp.float32)
        value_rows = lax.dynamic_index_in_dim(value_blocks, block_index, 0, keepdims=False).astype(jnp.float32)
        grad_rows = lax.dynamic_index_in_dim(grad_blocks, block_index, 0, keepdims=False).astype(jnp.float32)
        coarse_keys = [lax.dynamic_index_in_dim(key_levels[section], siblings[section], 0, keepdims=False) for section in range(LEVELS)]
        coarse_values = [lax.dynamic_index_in_dim(value_levels[section], siblings[section], 0, keepdims=False) for section in range(LEVELS)]
        key_set = jnp.concatenate([key_rows] + coarse_keys, axis=0)
        value_set = jnp.concatenate([value_rows] + coarse_values, axis=0)
        mixed, grad_query, grad_key, grad_value = attend(query_rows, key_set, value_set, grad_rows)
        new_keys = []
        new_values = []
        for section in range(LEVELS):
            begin = TOK_DEV + section * COARSE
            new_keys.append(key_grads[section].at[siblings[section]].add(grad_key[begin:begin + COARSE]))
            new_values.append(value_grads[section].at[siblings[section]].add(grad_value[begin:begin + COARSE]))
        return (new_keys, new_values), (mixed.astype(jnp.bfloat16), grad_query.astype(jnp.bfloat16),
                                        grad_key[:TOK_DEV], grad_value[:TOK_DEV])

    start = ([jnp.zeros_like(level) for level in key_levels], [jnp.zeros_like(level) for level in value_levels])
    carry, stacked = lax.scan(visit, start, jnp.arange(blocks, dtype=jnp.int32))
    key_grads, value_grads = carry
    key_grads = list(key_grads)
    value_grads = list(value_grads)
    for section in range(LEVELS - 1, 0, -1):
        key_grads[section - 1] = key_grads[section - 1] + spread_groups(key_grads[section])
        value_grads[section - 1] = value_grads[section - 1] + spread_groups(value_grads[section])

    def to_tokens(gradient):
        return jnp.broadcast_to(gradient[:, :, None, :] / pool_factor, (blocks, COARSE, pool_factor, D)).reshape(blocks, TOK_DEV, D)

    mixed, grad_query, fine_keys, fine_values = stacked
    grad_keys = (fine_keys + to_tokens(key_grads[0])).reshape(TOKENS, D).astype(jnp.bfloat16)
    grad_values = (fine_values + to_tokens(value_grads[0])).reshape(TOKENS, D).astype(jnp.bfloat16)
    return mixed.reshape(TOKENS, D), grad_query.reshape(TOKENS, D), grad_keys, grad_values
```

```python
import functools

import jax
import jax.numpy as jnp
import numpy as np
from jax import lax
from jax.experimental import pallas as pl
from jax.experimental.pallas import tpu as pltpu
from jax.sharding import PartitionSpec as P

F32 = jnp.float32
BF16 = jnp.bfloat16
D = 512
TOK = 256
PAIRS = 4
LANES = 128
SCALE = 64**-0.5
NT = (((1,), (1,)), ((), ()))
TN = (((0,), (0,)), ((), ()))


def flip(value, axis, mask):
    return lax.ppermute(value, axis, [(source, source ^ mask) for source in range(16)])


def reversed_bits(number, bits):
    return int(format(number, f"0{bits}b")[::-1], 2) if bits else 0


def token_pooling():
    table = np.zeros((104, TOK), np.float32)
    for base, bits in ((0, 6), (64, 5), (96, 3)):
        span = TOK >> bits
        for place in range(1 << bits):
            row = reversed_bits(place, bits)
            table[base + place, row * span : (row + 1) * span] = 1.0 / span
    return table


def group_pooling():
    table = np.zeros((64, 224), np.float32)

    def put(column, row, core, half, across, weight):
        table[row * 16 + core * 8 + half * 4 + across, column] = weight

    for core in range(2):
        for place in range(16):
            put(core * 16 + place, place % 4, core, 0, 0, 0.25)
            put(96 + core * 16 + place, place % 4, core, 0, 2, 0.25)
            put(128 + core * 16 + place, place % 4, core, 0, 3, 0.25)
        for place in range(32):
            put(32 + core * 32 + place, place % 4, core, 0, 1, 0.125)
        for across in range(4):
            for place in range(8):
                put(160 + across * 16 + core * 8 + place, place % 4, core, 1, across, 0.5)
    return table


def two_heads(block):
    first = lax.broadcasted_iota(jnp.int32, block.shape, 1) < 64
    zero = jnp.zeros_like(block)
    return jnp.concatenate([jnp.where(first, block, zero), jnp.where(first, zero, block)], axis=0)


def dot(left, right, dims=(((1,), (0,)), ((), ()))):
    return lax.dot_general(left, right, dims, preferred_element_type=F32)


def pool_kernel(table_ref, keys_ref, values_ref, zero_ref, one_ref, three_ref):
    for half, ref in enumerate((keys_ref, values_ref)):
        pooled = dot(table_ref[...], ref[...]).astype(BF16)
        columns = slice(half * D, (half + 1) * D)
        zero_ref[:, columns] = pooled[:64]
        one_ref[:, columns] = pooled[64:96]
        three_ref[:, columns] = pooled[96:104]


def stats_kernel(q_ref, do_ref, k_ref, v_ref, out_ref):
    q2 = two_heads(q_ref[...] * SCALE)
    d2 = two_heads(do_ref[...])
    scores = dot(k_ref[...], q2, NT)
    dprobs = dot(v_ref[...], d2, NT)
    largest = jnp.max(scores, axis=0, keepdims=True)
    expsc = jnp.exp(scores - largest)
    out_ref[0, 0:1] = largest
    out_ref[0, 1:2] = jnp.sum(expsc, axis=0, keepdims=True)
    out_ref[0, 2:3] = jnp.sum(expsc * dprobs, axis=0, keepdims=True)


def top_kernel(q_ref, do_ref, k_ref, v_ref, own_ref, low_ref, gk_ref, gv_ref, out_ref):
    q2 = two_heads(q_ref[...] * SCALE)
    d2 = two_heads(do_ref[...])
    scores = dot(k_ref[...], q2, NT)
    dprobs = dot(v_ref[...], d2, NT)
    own_largest, low_largest = own_ref[0, 0:1], low_ref[0, 0:1]
    largest = jnp.maximum(
        jnp.max(scores, axis=0, keepdims=True), jnp.maximum(own_largest, low_largest)
    )
    expsc = jnp.exp(scores - largest)
    own_part, low_part = jnp.exp(own_largest - largest), jnp.exp(low_largest - largest)
    total = (
        jnp.sum(expsc, axis=0, keepdims=True)
        + own_ref[0, 1:2] * own_part
        + low_ref[0, 1:2] * low_part
    )
    inner = (
        jnp.sum(expsc * dprobs, axis=0, keepdims=True)
        + own_ref[0, 2:3] * own_part
        + low_ref[0, 2:3] * low_part
    )
    share = 1.0 / total
    inner = inner * share
    out_ref[0, 0:1] = largest
    out_ref[0, 1:2] = share
    out_ref[0, 2:3] = inner
    probs = expsc * share
    dscores = (probs * (dprobs - inner)).astype(BF16)
    gk_ref[...] = dot(dscores, q2).astype(gk_ref.dtype)
    gv_ref[...] = dot(probs.astype(BF16), d2).astype(gv_ref.dtype)


def backward(q2, d2, k, v, stats_ref):
    scores = dot(k, q2, NT)
    dprobs = dot(v, d2, NT)
    probs = jnp.exp(scores - stats_ref[0, 0:1]) * stats_ref[0, 1:2]
    dscores = (probs * (dprobs - stats_ref[0, 2:3])).astype(BF16)
    weights = probs.astype(BF16)
    mixed_t = dot(v, weights, TN)
    gq_t = dot(k, dscores, TN)
    return weights, dscores, mixed_t, gq_t


def low_kernel(q_ref, do_ref, k_ref, v_ref, stats_ref, gk_ref, gv_ref, mixed_ref, gq_ref):
    q2 = two_heads(q_ref[...] * SCALE)
    d2 = two_heads(do_ref[...])
    weights, dscores, mixed_t, gq_t = backward(q2, d2, k_ref[...], v_ref[...], stats_ref)
    gk_ref[...] = dot(dscores, q2)
    gv_ref[...] = dot(weights, d2)
    mixed_ref[0] = mixed_t
    gq_ref[0] = gq_t


def own_kernel(
    q_ref, do_ref, k_ref, v_ref, tk_ref, tv_ref, stats_ref, low_mixed_ref, low_gq_ref,
    gk_ref, gv_ref, mixed_ref, gq_ref,
):
    q2 = two_heads(q_ref[...] * SCALE)
    d2 = two_heads(do_ref[...])
    weights, dscores, mixed_t, gq_t = backward(q2, d2, k_ref[...], v_ref[...], stats_ref)
    gk_ref[...] = dot(dscores, q2)
    gv_ref[...] = dot(weights, d2)
    unused_w, unused_d, top_mixed, top_gq = backward(q2, d2, tk_ref[...], tv_ref[...], stats_ref)

    def pick(both):
        return jnp.concatenate([both[:64, :TOK], both[64:, TOK:]], axis=0).T

    mixed_ref[...] = pick(mixed_t + top_mixed + low_mixed_ref[0]).astype(BF16)
    gq_ref[...] = pick((gq_t + top_gq + low_gq_ref[0]) * SCALE).astype(BF16)


def finish_kernel(table_ref, gk_ref, gv_ref, zero_ref, three_ref, keys_ref, values_ref):
    for half, (ref, out_ref) in enumerate(((gk_ref, keys_ref), (gv_ref, values_ref))):
        columns = slice(half * D, (half + 1) * D)
        rows = jnp.concatenate([zero_ref[:, columns], three_ref[:, columns].astype(F32)], axis=0)
        high = rows.astype(BF16)
        low = (rows - high.astype(F32)).astype(BF16)
        spread = dot(table_ref[...], high) + dot(table_ref[...], low)
        out_ref[...] = (ref[...] + spread).astype(BF16)


def rows_of_pair(rows, shift=0):
    return pl.BlockSpec((rows, LANES), lambda pair: (0, pair + shift))


def per_pair(rows, columns):
    return pl.BlockSpec((1, rows, columns), lambda pair: (pair, 0, 0))


STATS = jax.ShapeDtypeStruct((PAIRS, 8, 2 * TOK), F32)
STATS_SPEC = per_pair(8, 2 * TOK)
PARTIAL = jax.ShapeDtypeStruct((PAIRS, LANES, 2 * TOK), F32)
PARTIAL_SPEC = per_pair(LANES, 2 * TOK)
QUERY_SPECS = [rows_of_pair(TOK), rows_of_pair(TOK)]


def call(kernel, in_specs, out_specs, out_shape, flops, name):
    return pl.pallas_call(
        kernel,
        grid=(PAIRS,),
        in_specs=in_specs,
        out_specs=out_specs,
        out_shape=out_shape,
        compiler_params=pltpu.CompilerParams(vmem_limit_bytes=40 * 2**20),
        cost_estimate=pl.CostEstimate(flops=flops, bytes_accessed=2**20, transcendentals=0),
        name=name,
    )


def matmul_cost(keys, count):
    return 2 * count * keys * 2 * TOK * LANES * PAIRS


def own_stats(queries, cotangent, keys, values):
    return call(
        stats_kernel,
        QUERY_SPECS + [rows_of_pair(TOK), rows_of_pair(TOK)],
        STATS_SPEC, STATS, matmul_cost(TOK, 2), "own_stats",
    )(queries, cotangent, keys, values)


def low_stats(queries, cotangent, low):
    rows = low.shape[0]
    return call(
        stats_kernel,
        QUERY_SPECS + [rows_of_pair(rows), rows_of_pair(rows, PAIRS)],
        STATS_SPEC, STATS, matmul_cost(rows, 2), "low_stats",
    )(queries, cotangent, low, low)


def top_part(queries, cotangent, top, own, low):
    rows = top.shape[0]
    return call(
        top_kernel,
        QUERY_SPECS + [rows_of_pair(rows), rows_of_pair(rows, PAIRS), STATS_SPEC, STATS_SPEC],
        [rows_of_pair(rows), rows_of_pair(rows), STATS_SPEC],
        [jax.ShapeDtypeStruct((rows, D), BF16)] * 2 + [STATS],
        matmul_cost(rows, 4), "top_part",
    )(queries, cotangent, top, top, own, low)


def low_part(queries, cotangent, low, stats):
    rows = low.shape[0]
    return call(
        low_kernel,
        QUERY_SPECS + [rows_of_pair(rows), rows_of_pair(rows, PAIRS), STATS_SPEC],
        [rows_of_pair(rows), rows_of_pair(rows), PARTIAL_SPEC, PARTIAL_SPEC],
        [jax.ShapeDtypeStruct((rows, D), F32)] * 2 + [PARTIAL] * 2,
        matmul_cost(rows, 6), "low_part",
    )(queries, cotangent, low, low, stats)


def own_part(queries, cotangent, keys, values, top, stats, low_mixed, low_gq):
    rows = top.shape[0]
    return call(
        own_kernel,
        QUERY_SPECS
        + [rows_of_pair(TOK), rows_of_pair(TOK), rows_of_pair(rows), rows_of_pair(rows, PAIRS)]
        + [STATS_SPEC, PARTIAL_SPEC, PARTIAL_SPEC],
        [rows_of_pair(TOK)] * 4,
        [jax.ShapeDtypeStruct((TOK, D), F32)] * 2 + [jax.ShapeDtypeStruct((TOK, D), BF16)] * 2,
        matmul_cost(TOK, 6) + matmul_cost(rows, 4), "own_part",
    )(queries, cotangent, keys, values, top, top, stats, low_mixed, low_gq)


def whole(kernel, out_shape, name):
    return pl.pallas_call(kernel, out_shape=out_shape, name=name)


def halves(rows, parts=1):
    count, width = rows.shape
    split = rows.reshape(parts, 2, count // (2 * parts), width).astype(F32)
    return (0.5 * (split[:, 0] + split[:, 1])).astype(BF16).reshape(count // 2, width)


def spread(gradient, parts=1):
    count, width = gradient.shape
    split = (0.5 * gradient).reshape(parts, 1, count // parts, width)
    return jnp.concatenate([split, split], axis=1).reshape(2 * count, width)


def joined(*blocks):
    return jnp.concatenate(blocks, axis=0)


def shards(queries, keys, values, cotangent):
    pooling = token_pooling()
    grouping = group_pooling()
    wide = lambda rows: jax.ShapeDtypeStruct((rows, 2 * D), BF16)

    zero, one, three = whole(pool_kernel, [wide(64), wide(32), wide(8)], "pool")(
        jnp.asarray(pooling, BF16), keys, values
    )
    far = flip(three, "lo", 8)
    sec0 = flip(zero, "lo", 1)
    far_pair = joined(far, flip(far, "lo", 1))
    own = own_stats(queries, cotangent, keys, values)
    level1 = joined(one, halves(sec0))
    level2 = halves(level1, 2)
    short = joined(level2, far_pair)
    x1 = flip(joined(level1, far_pair), "lo", 2)
    x2 = flip(short, "lo", 4)
    x3 = flip(short, "lo", 6)
    sec3 = joined(far_pair, x1[64:], x2[32:], x3[32:])
    level4 = dot(
        jnp.asarray(grouping, BF16), joined(level2, x1[:64], x2[:32], x3[:32], sec3)
    ).astype(BF16)
    level5 = halves(level4)
    y1 = flip(level4, "hi", 1)
    y2 = flip(level5, "hi", 2)
    y3 = flip(level5, "hi", 3)
    level6 = joined(halves(level5), halves(halves(y1)), halves(y2), halves(y3))
    level7 = halves(level6, 4)
    low = joined(sec0, x1[:64], x2[:32], x3[:32], sec3, y1, y2, y3)
    z1 = flip(level6, "hi", 4)
    z2 = flip(level7, "hi", 8)
    z3 = flip(level7, "hi", 12)
    low_stat = low_stats(queries, cotangent, low)
    top = joined(z1, z2, z3)

    top_gk, top_gv, stats = top_part(queries, cotangent, top, own, low_stat)
    top_g = jnp.concatenate([top_gk, top_gv], axis=1)
    b1 = flip(top_g[:64], "hi", 4)
    b2 = flip(top_g[64:96], "hi", 8)
    b3 = flip(top_g[96:], "hi", 12)
    low_gk, low_gv, low_mixed, low_gq = low_part(queries, cotangent, low, stats)
    low_g = jnp.concatenate([low_gk, low_gv], axis=1)
    g6 = b1.astype(F32) + spread(b2.astype(F32) + b3.astype(F32), 4)
    b1 = flip((low_g[256:320] + spread(spread(g6[16:32]))).astype(BF16), "hi", 1)
    b2 = flip((low_g[320:352] + spread(g6[32:48])).astype(BF16), "hi", 2)
    b3 = flip((low_g[352:384] + spread(g6[48:64])).astype(BF16), "hi", 3)
    g5 = spread(g6[:16]) + b2.astype(F32) + b3.astype(F32)
    g4 = b1.astype(F32) + spread(g5)
    own_gk, own_gv, mixed, grad_queries = own_part(
        queries, cotangent, keys, values, top, stats, low_mixed, low_gq
    )
    g = dot(jnp.asarray(grouping.T, BF16), g4.astype(BF16))
    g3 = low_g[192:256] + g[160:224]
    b1 = flip(joined(low_g[64:128] + g[32:96], g3[16:32]).astype(BF16), "lo", 2)
    b2 = flip(joined(low_g[128:160] + g[96:128], g3[32:48]).astype(BF16), "lo", 4)
    b3 = flip(joined(low_g[160:192] + g[128:160], g3[48:64]).astype(BF16), "lo", 6)
    b1, b2, b3 = b1.astype(F32), b2.astype(F32), b3.astype(F32)
    g2 = g[:32] + b2[:32] + b3[:32]
    far_g = g3[:16] + b1[64:] + b2[32:] + b3[32:]
    g1 = b1[:64] + spread(g2, 2)
    back = flip(joined(low_g[:64] + spread(g1[32:]), far_g[8:]).astype(BF16), "lo", 1).astype(F32)
    g0 = back[:64] + spread(g1[:32])
    last = flip((far_g[:8] + back[64:]).astype(BF16), "lo", 8)
    unpool = np.concatenate([pooling[:64], pooling[96:]], axis=0).T
    grad_keys, grad_values = whole(
        finish_kernel, [jax.ShapeDtypeStruct((TOK, D), BF16)] * 2, "finish"
    )(jnp.asarray(unpool, BF16), own_gk, own_gv, g0, last)
    return (mixed, grad_queries, grad_keys, grad_values)


def solution(mesh):
    spec = P(("hi", "lo"), None)
    return jax.shard_map(
        shards, mesh=mesh, in_specs=(spec,) * 4, out_specs=(spec,) * 4, check_vma=False
    )
```

```python
import functools

import jax
import jax.numpy as jnp
import numpy as np
from jax import lax
from jax.experimental import pallas as pl
from jax.experimental.pallas import tpu as pltpu
from jax.sharding import PartitionSpec as P

F32 = jnp.float32
BF16 = jnp.bfloat16
D = 512
TOK = 256
PAIRS = 4
LANES = 128
SCALE = 64**-0.5
NT = (((1,), (1,)), ((), ()))
TN = (((0,), (0,)), ((), ()))


def flip(value, axis, mask):
    return lax.ppermute(value, axis, [(source, source ^ mask) for source in range(16)])


def reversed_bits(number, bits):
    return int(format(number, f"0{bits}b")[::-1], 2) if bits else 0


def token_pooling():
    table = np.zeros((104, TOK), np.float32)
    for base, bits in ((0, 6), (64, 5), (96, 3)):
        span = TOK >> bits
        for place in range(1 << bits):
            row = reversed_bits(place, bits) if bits > 3 else place
            table[base + place, row * span : (row + 1) * span] = 1.0 / span
    return table


def group_pooling():
    table = np.zeros((64, 224), np.float32)

    def put(column, row, core, half, across, weight):
        table[row * 16 + core * 8 + half * 4 + across, column] = weight

    for core in range(2):
        for place in range(16):
            put(core * 16 + place, place % 4, core, 0, 0, 0.25)
            put(96 + core * 16 + place, place % 4, core, 0, 2, 0.25)
            put(128 + core * 16 + place, place % 4, core, 0, 3, 0.25)
        for place in range(32):
            put(32 + core * 32 + place, place % 4, core, 0, 1, 0.125)
        for across in range(4):
            for place in range(8):
                row = reversed_bits(place >> 1, 2)
                put(160 + across * 16 + core * 8 + place, row, core, 1, across, 0.5)
    return table


def two_heads(block):
    first = lax.broadcasted_iota(jnp.int32, block.shape, 1) < 64
    zero = jnp.zeros_like(block)
    return jnp.concatenate([jnp.where(first, block, zero), jnp.where(first, zero, block)], axis=0)


def dot(left, right, dims=(((1,), (0,)), ((), ()))):
    return lax.dot_general(left, right, dims, preferred_element_type=F32)


def pool_kernel(table_ref, keys_ref, values_ref, zero_ref, one_ref, three_ref):
    for half, ref in enumerate((keys_ref, values_ref)):
        pooled = dot(table_ref[...], ref[...]).astype(BF16)
        columns = slice(half * D, (half + 1) * D)
        zero_ref[:, columns] = pooled[:64]
        one_ref[:, columns] = pooled[64:96]
        three_ref[:, columns] = pooled[96:104]


def stats_kernel(count, q_ref, do_ref, *refs):
    q2 = two_heads(q_ref[...] * SCALE)
    d2 = two_heads(do_ref[...])
    scores = jnp.concatenate([dot(ref[...], q2, NT) for ref in refs[:count]], axis=0)
    dprobs = jnp.concatenate([dot(ref[...], d2, NT) for ref in refs[count : 2 * count]], axis=0)
    out_ref = refs[-1]
    largest = jnp.max(scores, axis=0, keepdims=True)
    expsc = jnp.exp(scores - largest)
    out_ref[0, 0:1] = largest
    out_ref[0, 1:2] = jnp.sum(expsc, axis=0, keepdims=True)
    out_ref[0, 2:3] = jnp.sum(expsc * dprobs, axis=0, keepdims=True)


def top_kernel(q_ref, do_ref, k_ref, v_ref, low_ref, gk_ref, gv_ref, out_ref):
    q2 = two_heads(q_ref[...] * SCALE)
    d2 = two_heads(do_ref[...])
    scores = dot(k_ref[...], q2, NT)
    dprobs = dot(v_ref[...], d2, NT)
    low_largest = low_ref[0, 0:1]
    largest = jnp.maximum(jnp.max(scores, axis=0, keepdims=True), low_largest)
    expsc = jnp.exp(scores - largest)
    low_part = jnp.exp(low_largest - largest)
    total = jnp.sum(expsc, axis=0, keepdims=True) + low_ref[0, 1:2] * low_part
    inner = jnp.sum(expsc * dprobs, axis=0, keepdims=True) + low_ref[0, 2:3] * low_part
    share = 1.0 / total
    inner = inner * share
    out_ref[0, 0:1] = largest
    out_ref[0, 1:2] = share
    out_ref[0, 2:3] = inner
    probs = expsc * share
    dscores = (probs * (dprobs - inner)).astype(BF16)
    gk_ref[...] = dot(dscores, q2).astype(gk_ref.dtype)
    gv_ref[...] = dot(probs.astype(BF16), d2).astype(gv_ref.dtype)


def backward(q2, d2, k, v, stats_ref):
    scores = dot(k, q2, NT)
    dprobs = dot(v, d2, NT)
    probs = jnp.exp(scores - stats_ref[0, 0:1]) * stats_ref[0, 1:2]
    dscores = (probs * (dprobs - stats_ref[0, 2:3])).astype(BF16)
    weights = probs.astype(BF16)
    return weights, dscores, dot(v, weights, TN), dot(k, dscores, TN)


def grads_kernel(wanted, first, last, q_ref, do_ref, stats_ref, *refs):
    refs = list(refs)
    q2 = two_heads(q_ref[...] * SCALE)
    d2 = two_heads(do_ref[...])
    blocks = [(refs.pop(0), refs.pop(0)) for unused in wanted]
    before = [] if first else [refs.pop(0), refs.pop(0)]
    refs.pop(0)
    mixed_ref, gq_ref = refs.pop(0), refs.pop(0)
    mixed, gq = 0.0, 0.0
    for want, (k_ref, v_ref) in zip(wanted, blocks):
        weights, dscores, mixed_t, gq_t = backward(q2, d2, k_ref[...], v_ref[...], stats_ref)
        mixed, gq = mixed + mixed_t, gq + gq_t
        if want:
            gk_ref, gv_ref = refs.pop(0), refs.pop(0)
            gk_ref[...] = dot(dscores, q2)
            gv_ref[...] = dot(weights, d2)

    def pick(both):
        return jnp.concatenate([both[:64, :TOK], both[64:, TOK:]], axis=0)

    mixed, gq = pick(mixed), pick(gq)
    if before:
        mixed, gq = mixed + before[0][0], gq + before[1][0]
    if last:
        mixed_ref[...] = mixed.T.astype(BF16)
        gq_ref[...] = (gq * SCALE).T.astype(BF16)
    else:
        mixed_ref[0] = mixed
        gq_ref[0] = gq


def finish_kernel(table_ref, gk_ref, gv_ref, zero_ref, keys_ref, values_ref):
    for half, (ref, out_ref) in enumerate(((gk_ref, keys_ref), (gv_ref, values_ref))):
        rows = zero_ref[:, half * D : (half + 1) * D]
        high = rows.astype(BF16)
        low = (rows - high.astype(F32)).astype(BF16)
        out_ref[...] = ref[...] + dot(table_ref[...], high) + dot(table_ref[...], low)


def rows_of_pair(rows, shift=0):
    return pl.BlockSpec((rows, LANES), lambda pair: (0, pair + shift))


def per_pair(rows, columns):
    return pl.BlockSpec((1, rows, columns), lambda pair: (pair, 0, 0))


STATS = jax.ShapeDtypeStruct((PAIRS, 8, 2 * TOK), F32)
STATS_SPEC = per_pair(8, 2 * TOK)
PARTIAL = jax.ShapeDtypeStruct((PAIRS, LANES, TOK), F32)
PARTIAL_SPEC = per_pair(LANES, TOK)
QUERY_SPECS = [rows_of_pair(TOK), rows_of_pair(TOK)]


def call(kernel, in_specs, out_specs, out_shape, flops, name):
    return pl.pallas_call(
        kernel,
        grid=(PAIRS,),
        in_specs=in_specs,
        out_specs=out_specs,
        out_shape=out_shape,
        compiler_params=pltpu.CompilerParams(vmem_limit_bytes=40 * 2**20),
        cost_estimate=pl.CostEstimate(flops=flops, bytes_accessed=2**20, transcendentals=0),
        name=name,
    )


def matmul_cost(keys, count):
    return 2 * count * keys * 2 * TOK * LANES * PAIRS


def key_specs(block):
    keys, values = block
    return [rows_of_pair(keys.shape[0]), rows_of_pair(keys.shape[0], PAIRS if keys is values else 0)]


def low_stats(queries, cotangent, blocks):
    specs = [key_specs(block) for block in blocks]
    rows = sum(block[0].shape[0] for block in blocks)
    return call(
        functools.partial(stats_kernel, len(blocks)),
        QUERY_SPECS + [spec[0] for spec in specs] + [spec[1] for spec in specs],
        STATS_SPEC, STATS, matmul_cost(rows, 2), "low_stats",
    )(queries, cotangent, *[block[0] for block in blocks], *[block[1] for block in blocks])


def top_part(queries, cotangent, top, low):
    rows = top.shape[0]
    return call(
        top_kernel,
        QUERY_SPECS + key_specs((top, top)) + [STATS_SPEC],
        [rows_of_pair(rows), rows_of_pair(rows), STATS_SPEC],
        [jax.ShapeDtypeStruct((rows, D), BF16)] * 2 + [STATS],
        matmul_cost(rows, 4), "top_part",
    )(queries, cotangent, top, top, low)


def grads_part(queries, cotangent, stats, blocks, wanted, before, after, last, name):
    in_specs = QUERY_SPECS + [STATS_SPEC]
    operands = [queries, cotangent, stats]
    out_specs = [rows_of_pair(TOK)] * 2 if last else [PARTIAL_SPEC] * 2
    out_shape = [jax.ShapeDtypeStruct((TOK, D), BF16)] * 2 if last else [PARTIAL] * 2
    for block, want in zip(blocks, wanted):
        in_specs = in_specs + key_specs(block)
        operands += block
        if want:
            rows = block[0].shape[0]
            out_specs = out_specs + [rows_of_pair(rows)] * 2
            out_shape = out_shape + [jax.ShapeDtypeStruct((rows, D), F32)] * 2
    in_specs = in_specs + [PARTIAL_SPEC] * len(before) + [pl.BlockSpec((8, LANES), lambda pair: (0, 0))]
    operands += [*before, after]
    rows = sum(block[0].shape[0] for block in blocks)
    return call(
        functools.partial(grads_kernel, wanted, not before, last),
        in_specs, out_specs, out_shape, matmul_cost(rows, 6), name,
    )(*operands)


def whole(kernel, out_shape, name):
    return pl.pallas_call(kernel, out_shape=out_shape, name=name)


def halves(rows, parts=1):
    count, width = rows.shape
    split = rows.reshape(parts, 2, count // (2 * parts), width).astype(F32)
    return (0.5 * (split[:, 0] + split[:, 1])).astype(BF16).reshape(count // 2, width)


def spread(gradient, parts=1):
    count, width = gradient.shape
    split = (0.5 * gradient).reshape(parts, 1, count // parts, width)
    return jnp.concatenate([split, split], axis=1).reshape(2 * count, width)


def joined(*blocks):
    return jnp.concatenate(blocks, axis=0)


def both(gk, gv, rows=slice(None)):
    return jnp.concatenate([gk[rows], gv[rows]], axis=1)


def shards(queries, keys, values, cotangent):
    pooling = token_pooling()
    grouping = group_pooling()
    wide = lambda rows: jax.ShapeDtypeStruct((rows, 2 * D), BF16)

    zero, one, three = whole(pool_kernel, [wide(64), wide(32), wide(8)], "pool")(
        jnp.asarray(pooling, BF16), keys, values
    )
    far = flip(three, "lo", 8)
    sec0 = flip(zero, "lo", 1)
    far_pair = joined(far, flip(far, "lo", 1))
    level1 = joined(one, halves(sec0))
    level2 = halves(level1, 2)
    short = joined(level2, far_pair)
    x1 = flip(joined(level1, far_pair), "lo", 2)
    x2 = flip(short, "lo", 4)
    x3 = flip(short, "lo", 6)
    sec3 = joined(far_pair, x1[64:], x2[32:], x3[32:])
    low_x = joined(x1[:64], x2[:32], x3[:32], sec3)
    level4 = dot(jnp.asarray(grouping, BF16), joined(level2, low_x)).astype(BF16)
    level5 = halves(level4)
    y1 = flip(level4, "hi", 1)
    y2 = flip(level5, "hi", 2)
    y3 = flip(level5, "hi", 3)
    low_y = joined(y1, y2, y3)
    level6 = joined(halves(level5), halves(halves(y1)), halves(y2), halves(y3))
    level7 = halves(level6, 4)
    z1 = flip(level6, "hi", 4)
    z2 = flip(level7, "hi", 8)
    z3 = flip(level7, "hi", 12)
    own, sec0_block = (keys, values), (sec0, sec0)
    low = low_stats(queries, cotangent, [own, sec0_block, (low_x, low_x), (low_y, low_y)])
    top = joined(z1, z2, z3)

    top_gk, top_gv, stats = top_part(queries, cotangent, top, low)
    top_g = both(top_gk, top_gv)
    b1 = flip(top_g[:64], "hi", 4)
    b2 = flip(top_g[64:96], "hi", 8)
    b3 = flip(top_g[96:], "hi", 12)
    mixed, gq, gk, gv = grads_part(
        queries, cotangent, stats, [(low_y, low_y), (top, top)], (True, False), [], stats[0],
        False, "y_grads",
    )
    y_g = both(gk, gv)
    g6 = b1.astype(F32) + spread(b2.astype(F32) + b3.astype(F32), 4)
    b1 = flip((y_g[:64] + spread(spread(g6[16:32]))).astype(BF16), "hi", 1)
    b2 = flip((y_g[64:96] + spread(g6[32:48])).astype(BF16), "hi", 2)
    b3 = flip((y_g[96:] + spread(g6[48:64])).astype(BF16), "hi", 3)
    mixed, gq, gk, gv = grads_part(
        queries, cotangent, stats, [(low_x, low_x)], (True,), [mixed, gq], g6, False, "x_grads"
    )
    x_g = both(gk, gv)
    g5 = spread(g6[:16]) + b2.astype(F32) + b3.astype(F32)
    g4 = b1.astype(F32) + spread(g5)
    g = dot(jnp.asarray(grouping.T, BF16), g4.astype(BF16))
    x_g = x_g + g[32:]
    b1 = flip(joined(x_g[:64], x_g[144:160]).astype(BF16), "lo", 2)
    b2 = flip(joined(x_g[64:96], x_g[160:176]).astype(BF16), "lo", 4)
    b3 = flip(joined(x_g[96:128], x_g[176:]).astype(BF16), "lo", 6)
    mixed, grad_queries, gk, gv, own_gk, own_gv = grads_part(
        queries, cotangent, stats, [sec0_block, own], (True, True), [mixed, gq], g4, True, "own_grads"
    )
    b1, b2, b3 = b1.astype(F32), b2.astype(F32), b3.astype(F32)
    g2 = g[:32] + b2[:32] + b3[:32]
    far_g = x_g[128:144] + b1[64:] + b2[32:] + b3[32:]
    g1 = b1[:64] + spread(g2, 2)
    back = flip(joined(both(gk, gv) + spread(g1[32:]), far_g[8:]).astype(BF16), "lo", 1).astype(F32)
    g0 = back[:64] + spread(g1[:32])
    last = flip((far_g[:8] + back[64:]).astype(BF16), "lo", 8).astype(F32)
    near_keys, near_values = whole(
        finish_kernel, [jax.ShapeDtypeStruct((TOK, D), F32)] * 2, "finish"
    )(jnp.asarray(pooling[:64].T, BF16), own_gk, own_gv, g0)

    def add_last(near, part):
        blocks = near.reshape(8, TOK // 8, D) + (part * (8 / TOK))[:, None, :]
        return blocks.astype(BF16).reshape(TOK, D)

    return (mixed, grad_queries, add_last(near_keys, last[:, :D]), add_last(near_values, last[:, D:]))


def solution(mesh):
    spec = P(("hi", "lo"), None)
    return jax.shard_map(
        shards, mesh=mesh, in_specs=(spec,) * 4, out_specs=(spec,) * 4, check_vma=False
    )
```

```python
import functools

import jax
import jax.numpy as jnp
from jax import lax
from jax.experimental import pallas as pl
from jax.experimental.pallas import tpu as pltpu
from jax.sharding import PartitionSpec as P

F32 = jnp.float32
BF16 = jnp.bfloat16
D = 512
TOK = 256
PAIRS = 4
LANES = 128
SCALE = 64**-0.5
NT = (((1,), (1,)), ((), ()))
TN = (((0,), (0,)), ((), ()))


def flip(value, axis, mask):
    return lax.ppermute(value, axis, [(source, source ^ mask) for source in range(16)])


def reverse(number, bits):
    parts = [((number >> bit) & 1) << (bits - 1 - bit) for bit in range(bits)]
    return functools.reduce(jnp.bitwise_or, parts)


def iota(shape, dim):
    return lax.broadcasted_iota(jnp.int32, shape, dim)


def grouping(shape, row_dim):
    out, column = iota(shape, row_dim), iota(shape, 1 - row_dim)

    def choose(level2, x1, x2, x3, far):
        return jnp.where(
            column < 32, level2,
            jnp.where(column < 96, x1, jnp.where(column < 128, x2, jnp.where(column < 160, x3, far))),
        )

    place = column - choose(0, 32, 96, 128, 160)
    near, wide_core, far_core = place >> 4, place >> 5, (place >> 3) & 1
    core = choose(near, wide_core, near, near, far_core)
    row = jnp.where(column < 160, place & 3, reverse((place & 7) >> 1, 2))
    across = choose(0, 1, 2, 3, place >> 4)
    half = jnp.where(column < 160, 0, 1)
    weight = choose(0.25, 0.125, 0.25, 0.25, 0.5)
    return jnp.where(out == row * 16 + core * 8 + half * 4 + across, weight, 0.0).astype(BF16)


def two_heads(block):
    first = lax.broadcasted_iota(jnp.int32, block.shape, 1) < 64
    zero = jnp.zeros_like(block)
    return jnp.concatenate([jnp.where(first, block, zero), jnp.where(first, zero, block)], axis=0)


def dot(left, right, dims=(((1,), (0,)), ((), ()))):
    return lax.dot_general(left, right, dims, preferred_element_type=F32)


def pool_kernel(keys_ref, values_ref, zero_ref, one_ref, three_ref, keys, values, sems):
    moves = [
        pltpu.make_async_copy(source, target, sems.at[place])
        for place, (source, target) in enumerate(((keys_ref, keys), (values_ref, values)))
    ]
    for move in moves:
        move.start()
    place, token = iota((104, TOK), 0), iota((104, TOK), 1)
    row = jnp.where(place < 64, reverse(place, 6), jnp.where(place < 96, reverse(place, 5), place - 96))
    shift = jnp.where(place < 64, 2, jnp.where(place < 96, 3, 5))
    weight = jnp.where(place < 64, 1 / 4, jnp.where(place < 96, 1 / 8, 1 / 32))
    table = jnp.where((token >> shift) == row, weight, 0.0).astype(BF16)
    for half, (move, ref) in enumerate(zip(moves, (keys, values))):
        move.wait()
        pooled = dot(table, ref[...]).astype(BF16)
        columns = slice(half * D, (half + 1) * D)
        zero_ref[:, columns] = pooled[:64]
        one_ref[:, columns] = pooled[64:96]
        three_ref[:, columns] = pooled[96:104]


def group_kernel(level2_ref, far_ref, x1_ref, x2_ref, x3_ref, level4_ref, level5_ref, low_ref):
    low_ref[:64] = x1_ref[:64]
    low_ref[64:96] = x2_ref[:32]
    low_ref[96:128] = x3_ref[:32]
    low_ref[128:144] = far_ref[...]
    low_ref[144:160] = x1_ref[64:]
    low_ref[160:176] = x2_ref[32:]
    low_ref[176:] = x3_ref[32:]
    level4 = dot(grouping((64, 224), 0), jnp.concatenate([level2_ref[...], low_ref[...]], axis=0)).astype(BF16)
    level4_ref[...] = level4
    level5_ref[...] = (0.5 * (level4[:32].astype(F32) + level4[32:].astype(F32))).astype(BF16)


def pair_columns(index, step):
    return slice(index * LANES, (index + 1) * LANES)


def store_pair(ref, index, step, gk, gv):
    start = (pl.program_id(0) * step + index) * LANES
    ref[:, pl.ds(pl.multiple_of(start, LANES), LANES)] = gk.astype(ref.dtype)
    ref[:, pl.ds(pl.multiple_of(start + D, LANES), LANES)] = gv.astype(ref.dtype)


def stats_kernel(step, count, q_ref, do_ref, *refs):
    out_ref = refs[-1]
    for index in range(step):
        columns = pair_columns(index, step)
        q2 = two_heads(q_ref[:, columns] * SCALE)
        d2 = two_heads(do_ref[:, columns])
        scores = [dot(ref[:, columns], q2, NT) for ref in refs[:count]]
        dprobs = [dot(ref[:, columns], d2, NT) for ref in refs[count : 2 * count]]
        largest = functools.reduce(
            jnp.maximum, [jnp.max(part, axis=0, keepdims=True) for part in scores]
        )
        total, inner = 0.0, 0.0
        for score, dprob in zip(scores, dprobs):
            expsc = jnp.exp(score - largest)
            total = total + jnp.sum(expsc, axis=0, keepdims=True)
            inner = inner + jnp.sum(expsc * dprob, axis=0, keepdims=True)
        out_ref[index, 0:1] = largest
        out_ref[index, 1:2] = total
        out_ref[index, 2:3] = inner


def top_kernel(step, q_ref, do_ref, k_ref, v_ref, low_ref, g_ref, out_ref):
    for index in range(step):
        columns = pair_columns(index, step)
        q2 = two_heads(q_ref[:, columns] * SCALE)
        d2 = two_heads(do_ref[:, columns])
        scores = dot(k_ref[:, columns], q2, NT)
        dprobs = dot(v_ref[:, columns], d2, NT)
        low_largest = low_ref[index, 0:1]
        largest = jnp.maximum(jnp.max(scores, axis=0, keepdims=True), low_largest)
        expsc = jnp.exp(scores - largest)
        low_part = jnp.exp(low_largest - largest)
        total = jnp.sum(expsc, axis=0, keepdims=True) + low_ref[index, 1:2] * low_part
        inner = jnp.sum(expsc * dprobs, axis=0, keepdims=True) + low_ref[index, 2:3] * low_part
        share = 1.0 / total
        inner = inner * share
        out_ref[index, 0:1] = largest
        out_ref[index, 1:2] = share
        out_ref[index, 2:3] = inner
        probs = expsc * share
        dscores = (probs * (dprobs - inner)).astype(BF16)
        store_pair(g_ref, index, step, dot(dscores, q2), dot(probs.astype(BF16), d2))


def grads_kernel(step, wanted, first, last, q_ref, do_ref, stats_ref, *refs):
    refs = list(refs)
    blocks = [(refs.pop(0), refs.pop(0)) for unused in wanted]
    before = [] if first else [refs.pop(0), refs.pop(0)]
    refs.pop(0)
    mixed_ref, gq_ref = refs.pop(0), refs.pop(0)
    g_refs = [refs.pop(0) if want else None for want in wanted]
    for index in range(step):
        columns = pair_columns(index, step)
        q2 = two_heads(q_ref[:, columns] * SCALE)
        d2 = two_heads(do_ref[:, columns])
        mixed, gq = 0.0, 0.0
        for g_ref, (k_ref, v_ref) in zip(g_refs, blocks):
            k, v = k_ref[:, columns], v_ref[:, columns]
            probs = jnp.exp(dot(k, q2, NT) - stats_ref[index, 0:1]) * stats_ref[index, 1:2]
            dscores = (probs * (dot(v, d2, NT) - stats_ref[index, 2:3])).astype(BF16)
            weights = probs.astype(BF16)
            mixed, gq = mixed + dot(v, weights, TN), gq + dot(k, dscores, TN)
            if g_ref is not None:
                store_pair(g_ref, index, step, dot(dscores, q2), dot(weights, d2))

        def pick(both):
            return jnp.concatenate([both[:64, :TOK], both[64:, TOK:]], axis=0)

        mixed, gq = pick(mixed), pick(gq)
        if before:
            mixed, gq = mixed + before[0][index], gq + before[1][index]
        if last:
            mixed_ref[:, columns] = mixed.T.astype(BF16)
            gq_ref[:, columns] = (gq * SCALE).T.astype(BF16)
        else:
            mixed_ref[index] = mixed
            gq_ref[index] = gq


def ungroup_kernel(b1_ref, b2_ref, b3_ref, g6_ref, x_ref, x1_ref, x2_ref, x3_ref, level2_ref, far_ref):
    def doubled(rows):
        half = 0.5 * rows
        return jnp.concatenate([half, half], axis=0)

    g5 = doubled(g6_ref[:16]) + b2_ref[...].astype(F32) + b3_ref[...].astype(F32)
    g4 = b1_ref[...].astype(F32) + doubled(g5)
    g = dot(grouping((224, 64), 1), g4.astype(BF16))
    level2_ref[...] = g[:32]
    x = x_ref[...] + g[32:]
    x1_ref[:64] = x[:64].astype(BF16)
    x1_ref[64:] = x[144:160].astype(BF16)
    x2_ref[:32] = x[64:96].astype(BF16)
    x2_ref[32:] = x[160:176].astype(BF16)
    x3_ref[:32] = x[96:128].astype(BF16)
    x3_ref[32:] = x[176:].astype(BF16)
    far_ref[...] = x[128:144]


def finish_kernel(first_ref, second_ref, zero_ref, out_ref):
    place = reverse(iota((TOK, 64), 1), 6)
    unpooling = jnp.where((iota((TOK, 64), 0) >> 2) == place, 0.25, 0.0).astype(BF16)
    high = zero_ref[...].astype(BF16)
    low = (zero_ref[...] - high.astype(F32)).astype(BF16)
    for half, ref in enumerate((first_ref, second_ref)):
        rows = slice(half * TOK // 2, (half + 1) * TOK // 2)
        table = unpooling[rows]
        out_ref[rows] = ref[...] + dot(table, high) + dot(table, low)


def last_kernel(near_ref, part_ref, keys_ref, values_ref):
    part = part_ref[...].astype(F32) * (8 / TOK)
    for group in range(8):
        rows = slice(group * (TOK // 8), (group + 1) * (TOK // 8))
        total = (near_ref[rows] + part[group : group + 1]).astype(BF16)
        keys_ref[rows] = total[:, :D]
        values_ref[rows] = total[:, D:]


POOL_VMEM = 536 * 2**20 // 10
STEP = 2
TOP_STEP = 4


def of_pairs(rows, shift=0, step=STEP, part=0):
    return pl.BlockSpec((rows, LANES * step), lambda pair: (part, pair + shift // step))


def per_pair(rows, columns, step=STEP):
    return pl.BlockSpec((step, rows, columns), lambda pair: (pair, 0, 0))


def resident(rows, columns):
    return pl.BlockSpec((rows, columns), lambda pair: (0, 0))


STATS = jax.ShapeDtypeStruct((PAIRS, 8, 2 * TOK), F32)
PARTIAL = jax.ShapeDtypeStruct((PAIRS, LANES, TOK), F32)


def call(kernel, in_specs, out_specs, out_shape, flops, name, step=STEP):
    return pl.pallas_call(
        functools.partial(kernel, step),
        grid=(PAIRS // step,),
        in_specs=in_specs,
        out_specs=out_specs,
        out_shape=out_shape,
        compiler_params=pltpu.CompilerParams(vmem_limit_bytes=40 * 2**20),
        cost_estimate=pl.CostEstimate(flops=flops, bytes_accessed=2**20, transcendentals=0),
        name=name,
    )


def matmul_cost(keys, count):
    return 2 * count * keys * 2 * TOK * LANES * PAIRS


def key_specs(block, step=STEP, rows=None, part=0):
    keys, values = block
    shift = PAIRS if keys is values else 0
    rows = rows or keys.shape[0]
    return [of_pairs(rows, 0, step, part), of_pairs(rows, shift, step, part)]


def low_stats(queries, cotangent, blocks):
    specs = [key_specs(block) for block in blocks]
    rows = sum(block[0].shape[0] for block in blocks)

    def kernel(step, *refs):
        stats_kernel(step, len(blocks), *refs)

    return call(
        kernel,
        [of_pairs(TOK), of_pairs(TOK)]
        + [spec[0] for spec in specs]
        + [spec[1] for spec in specs],
        per_pair(8, 2 * TOK), STATS,
        matmul_cost(rows, 2), "low_stats",
    )(queries, cotangent, *[k for k, v in blocks], *[v for k, v in blocks])


def top_part(queries, cotangent, top, low):
    rows = top.shape[0]
    step = TOP_STEP
    return call(
        top_kernel,
        [of_pairs(TOK, 0, step), of_pairs(TOK, 0, step)]
        + key_specs((top, top), step)
        + [per_pair(8, 2 * TOK, step)],
        [resident(rows, 2 * D), per_pair(8, 2 * TOK, step)],
        [jax.ShapeDtypeStruct((rows, 2 * D), BF16), STATS],
        matmul_cost(rows, 4), "top_part", step,
    )(queries, cotangent, top, top, low)


def grads_part(queries, cotangent, stats, blocks, wanted, before, after, last, name):
    in_specs = [of_pairs(TOK), of_pairs(TOK), per_pair(8, 2 * TOK)]
    operands = [queries, cotangent, stats]
    out_specs = [of_pairs(TOK)] * 2 if last else [per_pair(LANES, TOK)] * 2
    out_shape = [jax.ShapeDtypeStruct((TOK, D), BF16)] * 2 if last else [PARTIAL] * 2
    total = 0
    for (keys, values, rows, part), want in zip(blocks, wanted):
        in_specs = in_specs + key_specs((keys, values), STEP, rows, part)
        operands += [keys, values]
        total += rows
        if want:
            out_specs = out_specs + [resident(rows, 2 * D)]
            out_shape = out_shape + [jax.ShapeDtypeStruct((rows, 2 * D), F32)]
    in_specs = in_specs + [per_pair(LANES, TOK)] * len(before) + [resident(8, LANES)]
    operands += [*before, after]

    def kernel(step, *refs):
        grads_kernel(step, wanted, not before, last, *refs)

    return call(kernel, in_specs, out_specs, out_shape, matmul_cost(total, 6), name)(*operands)


def wide(rows):
    return jax.ShapeDtypeStruct((rows, 2 * D), BF16)


def wide_f32(rows):
    return jax.ShapeDtypeStruct((rows, 2 * D), F32)


def pool(keys, values):
    return pl.pallas_call(
        pool_kernel,
        in_specs=[pl.BlockSpec(memory_space=pl.ANY)] * 2,
        out_specs=[pl.BlockSpec(memory_space=pltpu.VMEM)] * 3,
        out_shape=[wide(64), wide(32), wide(8)],
        scratch_shapes=[
            pltpu.VMEM((TOK, D), BF16),
            pltpu.VMEM((TOK, D), BF16),
            pltpu.SemaphoreType.DMA((2,)),
        ],
        compiler_params=pltpu.CompilerParams(vmem_limit_bytes=POOL_VMEM),
        name="pool",
    )(keys, values)


def whole(kernel, out_shape, name):
    return pl.pallas_call(
        kernel,
        out_shape=out_shape,
        compiler_params=pltpu.CompilerParams(vmem_limit_bytes=16 * 2**20),
        name=name,
    )


def halves(rows, parts=1):
    count, width = rows.shape
    split = rows.reshape(parts, 2, count // (2 * parts), width).astype(F32)
    return (0.5 * (split[:, 0] + split[:, 1])).astype(BF16).reshape(count // 2, width)


def spread(gradient, parts=1):
    count, width = gradient.shape
    split = (0.5 * gradient).reshape(parts, 1, count // parts, width)
    return jnp.concatenate([split, split], axis=1).reshape(2 * count, width)


def joined(*blocks):
    return jnp.concatenate(blocks, axis=0)


def shards(queries, keys, values, cotangent):
    zero, one, three = pool(keys, values)
    far = flip(three, "lo", 8)
    sec0 = flip(zero, "lo", 1)
    far_pair = joined(far, flip(far, "lo", 1))
    level1 = joined(one, halves(sec0))
    level2 = halves(level1, 2)
    short = joined(level2, far_pair)
    x1 = flip(joined(level1, far_pair), "lo", 2)
    x2 = flip(short, "lo", 4)
    x3 = flip(short, "lo", 6)
    level4, level5, low_x = whole(group_kernel, [wide(64), wide(32), wide(192)], "group")(
        level2, far_pair, x1, x2, x3
    )
    y1 = flip(level4, "hi", 1)
    y2 = flip(level5, "hi", 2)
    y3 = flip(level5, "hi", 3)
    low_y = joined(y1, y2, y3)
    level6 = joined(halves(level5), halves(halves(y1)), halves(y2), halves(y3))
    level7 = halves(level6, 4)
    z1 = flip(level6, "hi", 4)
    z2 = flip(level7, "hi", 8)
    z3 = flip(level7, "hi", 12)
    own, sec0_block = (keys, values), (sec0, sec0)
    low = low_stats(queries, cotangent, [own, sec0_block, (low_x, low_x), (low_y, low_y)])
    top = joined(z1, z2, z3)

    top_g, stats = top_part(queries, cotangent, top, low)
    b1 = flip(top_g[:64], "hi", 4)
    b2 = flip(top_g[64:96], "hi", 8)
    b3 = flip(top_g[96:], "hi", 12)
    mixed, gq, y_g = grads_part(
        queries, cotangent, stats, [(low_y, low_y, 128, 0), (top, top, 128, 0)], (True, False), [], stats[0],
        False, "y_grads",
    )
    g6 = b1.astype(F32) + spread(b2.astype(F32) + b3.astype(F32), 4)
    b1 = flip((y_g[:64] + spread(spread(g6[16:32]))).astype(BF16), "hi", 1)
    b2 = flip((y_g[64:96] + spread(g6[32:48])).astype(BF16), "hi", 2)
    b3 = flip((y_g[96:] + spread(g6[48:64])).astype(BF16), "hi", 3)
    mixed, gq, x_g, own_g = grads_part(
        queries, cotangent, stats,
        [(low_x, low_x, 192, 0), (keys, values, TOK // 2, 0)], (True,) * 2,
        [mixed, gq], g6, False, "x_grads",
    )
    x1, x2, x3, level2_g, far_g = whole(
        ungroup_kernel, [wide(80), wide(48), wide(48), wide_f32(32), wide_f32(16)], "ungroup"
    )(b1, b2, b3, g6, x_g)
    b1 = flip(x1, "lo", 2)
    b2 = flip(x2, "lo", 4)
    b3 = flip(x3, "lo", 6)
    mixed, grad_queries, sec0_g, rest_g = grads_part(
        queries, cotangent, stats, [(sec0, sec0, 64, 0), (keys, values, TOK // 2, 1)],
        (True,) * 2, [mixed, gq], far_g, True, "own_grads",
    )
    b1, b2, b3 = b1.astype(F32), b2.astype(F32), b3.astype(F32)
    g2 = level2_g + b2[:32] + b3[:32]
    far_g = far_g + b1[64:] + b2[32:] + b3[32:]
    g1 = b1[:64] + spread(g2, 2)
    back = flip(joined(sec0_g + spread(g1[32:]), far_g[8:]).astype(BF16), "lo", 1).astype(F32)
    g0 = back[:64] + spread(g1[:32])
    last = flip((far_g[:8] + back[64:]).astype(BF16), "lo", 8)
    near = whole(finish_kernel, jax.ShapeDtypeStruct((TOK, 2 * D), F32), "finish")(
        own_g, rest_g, g0
    )
    grad_keys, grad_values = whole(
        last_kernel, [jax.ShapeDtypeStruct((TOK, D), BF16)] * 2, "add_last"
    )(near, last)
    return (mixed, grad_queries, grad_keys, grad_values)


def solution(mesh):
    spec = P(("hi", "lo"), None)
    return jax.shard_map(
        shards, mesh=mesh, in_specs=(spec,) * 4, out_specs=(spec,) * 4, check_vma=False
    )
```

```python
import functools

import jax
import jax.numpy as jnp
from jax import lax
from jax.experimental import pallas as pl
from jax.experimental.pallas import tpu as pltpu
from jax.sharding import PartitionSpec as P

F32 = jnp.float32
BF16 = jnp.bfloat16
D = 512
TOK = 256
PAIRS = 4
LANES = 128
SCALE = 64**-0.5
NT = (((1,), (1,)), ((), ()))
TN = (((0,), (0,)), ((), ()))


def flip(value, axis, mask):
    return lax.ppermute(value, axis, [(source, source ^ mask) for source in range(16)])


def reverse(number, bits):
    parts = [((number >> bit) & 1) << (bits - 1 - bit) for bit in range(bits)]
    return functools.reduce(jnp.bitwise_or, parts)


def iota(shape, dim):
    return lax.broadcasted_iota(jnp.int32, shape, dim)


def grouping(shape, row_dim):
    out, column = iota(shape, row_dim), iota(shape, 1 - row_dim)

    def choose(level2, x1, x2, x3, far):
        return jnp.where(
            column < 16, level2,
            jnp.where(column < 48, x1, jnp.where(column < 64, x2, jnp.where(column < 80, x3, far))),
        )

    place = column - choose(0, 16, 48, 64, 80)
    row = jnp.where(column < 80, place & 3, reverse((place & 7) >> 1, 2))
    across = choose(0, 1, 2, 3, place >> 3)
    half = jnp.where(column < 80, 0, 1)
    weight = choose(0.25, 0.125, 0.25, 0.25, 0.5)
    return jnp.where(out == row * 8 + half * 4 + across, weight, 0.0).astype(BF16)


def two_heads(block):
    first = lax.broadcasted_iota(jnp.int32, block.shape, 1) < 64
    zero = jnp.zeros_like(block)
    return jnp.concatenate([jnp.where(first, block, zero), jnp.where(first, zero, block)], axis=0)


def dot(left, right, dims=(((1,), (0,)), ((), ()))):
    return lax.dot_general(left, right, dims, preferred_element_type=F32)


def pool_kernel(keys_ref, values_ref, zero_ref, one_ref, two_ref, three_ref, keys, values, sems):
    moves = [
        pltpu.make_async_copy(source, target, sems.at[place])
        for place, (source, target) in enumerate(((keys_ref, keys), (values_ref, values)))
    ]
    for move in moves:
        move.start()
    place, token = iota((128, TOK), 0), iota((128, TOK), 1)

    def choose(zero, one, two, three):
        return jnp.where(
            place < 64, zero, jnp.where(place < 96, one, jnp.where(place < 112, two, three))
        )

    row = choose(reverse(place, 6), reverse(place, 5), reverse(place, 4), place - 112)
    weight = choose(1 / 4, 1 / 8, 1 / 16, 1 / 32)
    table = jnp.where((token >> choose(2, 3, 4, 5)) == row, weight, 0.0).astype(BF16)
    for half, (move, ref) in enumerate(zip(moves, (keys, values))):
        move.wait()
        pooled = dot(table, ref[...]).astype(BF16)
        columns = slice(half * D, (half + 1) * D)
        zero_ref[:, columns] = pooled[:64]
        one_ref[:, columns] = pooled[64:96]
        two_ref[:, columns] = pooled[96:112]
        three_ref[:, columns] = pooled[112:120]


def doubled(rows):
    half = 0.5 * rows
    return jnp.concatenate([half, half], axis=0)


def near_kernel(z3_ref, z2_ref, z1_ref, after_ref, out_ref):
    out_ref[:32] = z1_ref[...]
    out_ref[32:64] = z2_ref[...]
    out_ref[64:] = z3_ref[...]


def level6_kernel(level5_ref, y3_ref, y2_ref, y1_ref, low_ref, level6_ref):
    low_ref[:32] = y1_ref[...]
    low_ref[32:48] = y2_ref[...]
    low_ref[48:] = y3_ref[...]
    level6_ref[:8] = pair_mean(level5_ref[...])
    level6_ref[8:16] = pair_mean(pair_mean(y1_ref[...]))
    level6_ref[16:24] = pair_mean(y2_ref[...])
    level6_ref[24:] = pair_mean(y3_ref[...])


def pair_mean(rows):
    half = rows.shape[0] // 2
    return (0.5 * (rows[:half].astype(F32) + rows[half:].astype(F32))).astype(BF16)


def group_kernel(two_ref, far_ref, x3_ref, x2_ref, x1_ref, level4_ref, level5_ref, low_ref):
    low_ref[:32] = x1_ref[:32]
    low_ref[32:48] = x2_ref[:16]
    low_ref[48:64] = x3_ref[:16]
    low_ref[64:72] = far_ref[...]
    low_ref[72:80] = x1_ref[32:]
    low_ref[80:88] = x2_ref[16:]
    low_ref[88:] = x3_ref[16:]
    level4 = dot(grouping((32, 112), 0), jnp.concatenate([two_ref[...], low_ref[...]], axis=0)).astype(BF16)
    level4_ref[...] = level4
    level5_ref[...] = (0.5 * (level4[:16].astype(F32) + level4[16:].astype(F32))).astype(BF16)


def y_send_kernel(b3_ref, b2_ref, b1_ref, own_ref, other_ref, y1_ref, y2_ref, y3_ref, g6_ref):
    shared = 0.5 * (b2_ref[...].astype(F32) + b3_ref[...].astype(F32))
    for core, y_ref in enumerate((own_ref, other_ref)):
        wide_rows, rows = slice(core * 32, core * 32 + 32), slice(core * 16, core * 16 + 16)
        g6 = b1_ref[wide_rows].astype(F32) + shared
        g6_ref[wide_rows] = g6
        y1_ref[wide_rows] = (y_ref[:32] + doubled(doubled(g6[8:16]))).astype(BF16)
        y2_ref[rows] = (y_ref[32:48] + doubled(g6[16:24])).astype(BF16)
        y3_ref[rows] = (y_ref[48:] + doubled(g6[24:])).astype(BF16)


def x_send_kernel(b3_ref, b2_ref, b1_ref, g6_ref, own_ref, other_ref, x1_ref, x2_ref, x3_ref, two_ref, far_ref
):
    table = grouping((112, 32), 1)
    for core, x_ref in enumerate((own_ref, other_ref)):
        wide_rows, rows = slice(core * 32, core * 32 + 32), slice(core * 16, core * 16 + 16)
        g5 = doubled(g6_ref[core * 32 : core * 32 + 8])
        g5 = g5 + b2_ref[rows].astype(F32) + b3_ref[rows].astype(F32)
        g = dot(table, (b1_ref[wide_rows].astype(F32) + doubled(g5)).astype(BF16))
        two_ref[rows] = g[:16]
        x = x_ref[...] + g[16:]
        far = slice(core * 8, core * 8 + 8)
        x1_ref[wide_rows] = x[:32].astype(BF16)
        x1_ref[64 + core * 8 : 72 + core * 8] = x[72:80].astype(BF16)
        for ref, first, second in ((x2_ref, 32, 80), (x3_ref, 48, 88)):
            ref[rows] = x[first : first + 16].astype(BF16)
            ref[32 + core * 8 : 40 + core * 8] = x[second : second + 8].astype(BF16)
        far_ref[far] = x[64:72]


def core_send_kernel(b3_ref, b2_ref, b1_ref, two_ref, far_ref, zero_ref, out_ref, one_ref, own_far_ref):
    for core in range(2):
        wide_rows, rows = slice(core * 32, core * 32 + 32), slice(core * 16, core * 16 + 16)
        near, far = slice(core * 8, core * 8 + 8), slice(32 + core * 8, 40 + core * 8)
        two = two_ref[rows] + b2_ref[rows].astype(F32) + b3_ref[rows].astype(F32)
        one = doubled(b1_ref[wide_rows].astype(F32) + doubled(two))
        last = b2_ref[far].astype(F32) + b3_ref[far].astype(F32)
        last = last + far_ref[near] + b1_ref[64 + core * 8 : 72 + core * 8].astype(F32)
        if core == 0:
            one_ref[...] = one
            own_far_ref[...] = last
        else:
            out_ref[:64] = (zero_ref[...] + one).astype(BF16)
            out_ref[64:] = last.astype(BF16)


def of_pair(ref, pair, rows=slice(None), shift=0):
    return ref[rows, shift + pair * LANES : shift + (pair + 1) * LANES]


def of_block(refs, pair, rows):
    return of_pair(refs[0], pair, rows), of_pair(refs[-1], pair, rows, 2 * D // len(refs) - D)


def of_blocks(blocks, pair, rows):
    parts = [of_block(block, pair, part) for block, part in zip(blocks, rows)]
    return [jnp.concatenate(side, axis=0) for side in zip(*parts)]


def store_pair(ref, pair, gk, gv):
    ref[:, pair * LANES : (pair + 1) * LANES] = gk.astype(ref.dtype)
    ref[:, D + pair * LANES : D + (pair + 1) * LANES] = gv.astype(ref.dtype)


def take(refs, counts):
    refs = iter(refs)
    return [[next(refs) for unused in range(count)] for count in counts]


def stats_kernel(counts, q_ref, do_ref, *refs):
    out_ref = refs[-1]
    blocks = take(refs, counts)
    for pair in range(PAIRS):
        q2 = two_heads(of_pair(q_ref, pair) * SCALE)
        d2 = two_heads(of_pair(do_ref, pair))
        k, v = of_blocks(blocks, pair, [slice(None)] * len(blocks))
        scores = dot(k, q2, NT)
        largest = jnp.max(scores, axis=0, keepdims=True)
        expsc = jnp.exp(scores - largest)
        out_ref[pair, 0:1] = largest
        out_ref[pair, 1:2] = jnp.sum(expsc, axis=0, keepdims=True)
        out_ref[pair, 2:3] = jnp.sum(expsc * dot(v, d2, NT), axis=0, keepdims=True)


def top_kernel(q_ref, do_ref, top_ref, low_ref, z1_ref, z2_ref, z3_ref, out_ref):
    for pair in range(PAIRS):
        q2 = two_heads(of_pair(q_ref, pair) * SCALE)
        d2 = two_heads(of_pair(do_ref, pair))
        k, v = of_block([top_ref], pair, slice(None))
        scores = dot(k, q2, NT)
        dprobs = dot(v, d2, NT)
        low_largest = low_ref[pair, 0:1]
        largest = jnp.maximum(jnp.max(scores, axis=0, keepdims=True), low_largest)
        expsc = jnp.exp(scores - largest)
        low_part = jnp.exp(low_largest - largest)
        total = jnp.sum(expsc, axis=0, keepdims=True) + low_ref[pair, 1:2] * low_part
        inner = jnp.sum(expsc * dprobs, axis=0, keepdims=True) + low_ref[pair, 2:3] * low_part
        share = 1.0 / total
        inner = inner * share
        out_ref[pair, 0:1] = largest
        out_ref[pair, 1:2] = share
        out_ref[pair, 2:3] = inner
        probs = expsc * share
        dscores = (probs * (dprobs - inner)).astype(BF16)
        gk, gv = dot(dscores, q2), dot(probs.astype(BF16), d2)
        store_pair(z1_ref, pair, gk[:64], gv[:64])
        store_pair(z2_ref, pair, gk[64:96], gv[64:96])
        store_pair(z3_ref, pair, gk[96:], gv[96:])


def grads_kernel(counts, rows, first, last, q_ref, do_ref, stats_ref, *refs):
    blocks = take(refs, counts)
    rest = list(refs[sum(counts) :])
    before = [] if first else [rest.pop(0), rest.pop(0)]
    rest.pop(0)
    mixed_ref, gq_ref = rest.pop(0), rest.pop(0)
    g_refs = rest
    for pair in range(PAIRS):
        q2 = two_heads(of_pair(q_ref, pair) * SCALE)
        d2 = two_heads(of_pair(do_ref, pair))
        k, v = of_blocks(blocks, pair, rows)
        probs = jnp.exp(dot(k, q2, NT) - stats_ref[pair, 0:1]) * stats_ref[pair, 1:2]
        dscores = (probs * (dot(v, d2, NT) - stats_ref[pair, 2:3])).astype(BF16)
        weights = probs.astype(BF16)
        mixed, gq = dot(v, weights, TN), dot(k, dscores, TN)
        count = sum(ref.shape[0] for ref in g_refs)
        gk, gv, start = dot(dscores[:count], q2), dot(weights[:count], d2), 0
        for ref in g_refs:
            store_pair(ref, pair, gk[start : start + ref.shape[0]], gv[start : start + ref.shape[0]])
            start += ref.shape[0]

        def pick(both):
            return jnp.concatenate([both[:64, :TOK], both[64:, TOK:]], axis=0)

        mixed, gq = pick(mixed), pick(gq)
        if before:
            mixed, gq = mixed + before[0][pair], gq + before[1][pair]
        if last:
            columns = slice(pair * LANES, (pair + 1) * LANES)
            mixed_ref[:, columns] = mixed.T.astype(BF16)
            gq_ref[:, columns] = (gq * SCALE).T.astype(BF16)
        else:
            mixed_ref[pair] = mixed
            gq_ref[pair] = gq


def finish_kernel(first_ref, second_ref, zero_ref, out_ref):
    place = reverse(iota((TOK, 64), 1), 6)
    unpooling = jnp.where((iota((TOK, 64), 0) >> 2) == place, 0.25, 0.0).astype(BF16)
    high = zero_ref[...].astype(BF16)
    low = (zero_ref[...] - high.astype(F32)).astype(BF16)
    for half, ref in enumerate((first_ref, second_ref)):
        rows = slice(half * TOK // 2, (half + 1) * TOK // 2)
        table = unpooling[rows]
        out_ref[rows] = ref[...] + dot(table, high) + dot(table, low)


def last_kernel(near_ref, part_ref, keys_ref, values_ref):
    part = part_ref[...].astype(F32) * (8 / TOK)
    for group in range(8):
        rows = slice(group * (TOK // 8), (group + 1) * (TOK // 8))
        total = (near_ref[rows] + part[group : group + 1]).astype(BF16)
        keys_ref[rows] = total[:, :D]
        values_ref[rows] = total[:, D:]


POOL_VMEM = 536 * 2**20 // 10
STATS = jax.ShapeDtypeStruct((PAIRS, 8, 2 * TOK), F32)
PARTIAL = jax.ShapeDtypeStruct((PAIRS, LANES, TOK), F32)


def call(kernel, operands, out_shape, flops, name, ordered=False):
    in_specs = [pl.BlockSpec(memory_space=pltpu.VMEM)] * len(operands)
    if ordered:
        in_specs[-1] = pl.BlockSpec(memory_space=pl.ANY)
    return pl.pallas_call(
        kernel,
        in_specs=in_specs,
        out_shape=out_shape,
        compiler_params=pltpu.CompilerParams(vmem_limit_bytes=40 * 2**20),
        cost_estimate=pl.CostEstimate(flops=flops, bytes_accessed=2**20, transcendentals=0),
        name=name,
    )(*operands)


def matmul_cost(keys, count):
    return 2 * count * keys * 2 * TOK * LANES * PAIRS


def low_stats(queries, cotangent, blocks):
    return call(
        functools.partial(stats_kernel, [len(block) for block in blocks]),
        [queries, cotangent] + [array for block in blocks for array in block],
        STATS, matmul_cost(5 * LANES, 2), "low_stats",
    )


def top_part(queries, cotangent, top, low):
    rows = top.shape[0]
    return call(
        top_kernel, [queries, cotangent, top, low], [wide(64), wide(32), wide(32), STATS],
        matmul_cost(rows, 4), "top_part",
    )


def grads_part(queries, cotangent, stats, blocks, wanted, before, after, last, name):
    operands = [queries, cotangent, stats]
    out_shape = [jax.ShapeDtypeStruct((TOK, D), BF16)] * 2 if last else [PARTIAL] * 2
    counts, rows, total = [], [], 0
    for (arrays, start, size), want in zip(blocks, wanted):
        operands += arrays
        counts.append(len(arrays))
        rows.append(slice(start, start + size))
        total += size
        if want:
            out_shape = out_shape + [jax.ShapeDtypeStruct((size, 2 * D), want)]
    return call(
        functools.partial(grads_kernel, counts, rows, not before, last),
        operands + [*before, after], out_shape, matmul_cost(total, 6), name, True,
    )


def wide(rows):
    return jax.ShapeDtypeStruct((rows, 2 * D), BF16)


def wide_f32(rows):
    return jax.ShapeDtypeStruct((rows, 2 * D), F32)


def pool(keys, values):
    return pl.pallas_call(
        pool_kernel,
        in_specs=[pl.BlockSpec(memory_space=pl.ANY)] * 2,
        out_specs=[pl.BlockSpec(memory_space=pltpu.VMEM)] * 4,
        out_shape=[wide(64), wide(32), wide(16), wide(8)],
        scratch_shapes=[
            pltpu.VMEM((TOK, D), BF16),
            pltpu.VMEM((TOK, D), BF16),
            pltpu.SemaphoreType.DMA((2,)),
        ],
        compiler_params=pltpu.CompilerParams(vmem_limit_bytes=POOL_VMEM),
        name="pool",
    )(keys, values)


def whole(kernel, out_shape, name, ordered=None):
    extra = {} if ordered is None else {
        "in_specs": [pl.BlockSpec(memory_space=pltpu.VMEM)] * ordered + [pl.BlockSpec(memory_space=pl.ANY)]
    }
    return pl.pallas_call(
        kernel,
        out_shape=out_shape,
        compiler_params=pltpu.CompilerParams(vmem_limit_bytes=16 * 2**20),
        name=name,
        **extra,
    )


def mean(one, two):
    return (0.5 * (one.astype(F32) + two.astype(F32))).astype(BF16)


def joined(*blocks):
    return jnp.concatenate(blocks, axis=0)


def other_core(value):
    return flip(value, "lo", 1)


def shards(queries, keys, values, cotangent):
    zero, one, two, three = pool(keys, values)
    far = flip(three, "lo", 8)
    sec0 = other_core(zero)
    short = joined(two, far)
    x1 = flip(joined(one, far), "lo", 2)
    x2 = flip(short, "lo", 4)
    x3 = flip(short, "lo", 6)
    level4, level5, low_x = whole(group_kernel, [wide(32), wide(16), wide(96)], "group")(
        two, far, x3, x2, x1
    )
    y1 = flip(level4, "hi", 1)
    y2 = flip(level5, "hi", 2)
    y3 = flip(level5, "hi", 3)
    low_x2 = other_core(low_x)
    low_y, level6 = whole(level6_kernel, [wide(64), wide(32)], "level6")(level5, y3, y2, y1)
    z1 = flip(level6, "hi", 4)
    z2 = flip(level6, "hi", 8)
    z3 = flip(level6, "hi", 12)
    low_y2 = other_core(low_y)
    low = low_stats(
        queries, cotangent,
        [(keys, values)] + [(rows,) for rows in (sec0, low_x, low_x2, low_y, low_y2)],
    )
    near = whole(near_kernel, wide(96), "near", 3)(z3, z2, z1, low)
    mate = other_core(near)
    top = joined(near[:32], mate[:32], mean(near[32:], mate[32:]))

    z1, z2, z3, stats = top_part(queries, cotangent, top, low)
    b1 = flip(z1, "hi", 4)
    b2 = flip(z2, "hi", 8)
    b3 = flip(z3, "hi", 12)
    mixed, gq, y_g, y_other = grads_part(
        queries, cotangent, stats, [([low_y], 0, 64), ([low_y2], 0, 64), ([top], 0, 128)],
        (F32, F32, None), [], z1, False, "y_grads",
    )
    y1, y2, y3, g6 = whole(y_send_kernel, [wide(64), wide(32), wide(32), wide_f32(64)], "y_send")(
        b3, b2, b1, y_g, y_other
    )
    b1 = flip(y1, "hi", 1)
    b2 = flip(y2, "hi", 2)
    b3 = flip(y3, "hi", 3)
    mixed, gq, x_g, x_other, first_g = grads_part(
        queries, cotangent, stats,
        [([low_x], 0, 96), ([low_x2], 0, 96), ([keys, values], 0, TOK // 2)],
        (F32,) * 3, [mixed, gq], y1, False, "x_grads",
    )
    x1, x2, x3, two_g, far_g = whole(
        x_send_kernel, [wide(80), wide(48), wide(48), wide_f32(32), wide_f32(16)], "x_send"
    )(b3, b2, b1, g6, x_g, x_other)
    b1 = flip(x1, "lo", 2)
    b2 = flip(x2, "lo", 4)
    b3 = flip(x3, "lo", 6)
    mixed, grad_queries, sec0_g, second_g = grads_part(
        queries, cotangent, stats, [([sec0], 0, 64), ([keys, values], TOK // 2, TOK // 2)],
        (F32,) * 2, [mixed, gq], x1, True, "own_grads",
    )
    mate_g, one_g, far_g = whole(core_send_kernel, [wide(72), wide_f32(64), wide_f32(8)], "core_send")(
        b3, b2, b1, two_g, far_g, sec0_g
    )
    back = other_core(mate_g).astype(F32)
    last = flip((far_g + back[64:]).astype(BF16), "lo", 8)
    near = whole(finish_kernel, jax.ShapeDtypeStruct((TOK, 2 * D), F32), "finish")(
        first_g, second_g, back[:64] + one_g
    )
    grad_keys, grad_values = whole(
        last_kernel, [jax.ShapeDtypeStruct((TOK, D), BF16)] * 2, "add_last"
    )(near, last)
    return (mixed, grad_queries, grad_keys, grad_values)


def solution(mesh):
    spec = P(("hi", "lo"), None)
    return jax.shard_map(
        shards, mesh=mesh, in_specs=(spec,) * 4, out_specs=(spec,) * 4, check_vma=False
    )
```

```python
import functools

import jax
import jax.numpy as jnp
from jax import lax
from jax.experimental import pallas as pl
from jax.experimental.pallas import tpu as pltpu
from jax.sharding import PartitionSpec as P

F32 = jnp.float32
BF16 = jnp.bfloat16
D = 512
TOK = 256
PAIRS = 4
LANES = 128
SCALE = 64**-0.5
NT = (((1,), (1,)), ((), ()))
TN = (((0,), (0,)), ((), ()))


def flip(value, axis, mask):
    return lax.ppermute(value, axis, [(source, source ^ mask) for source in range(16)])


def reverse(number, bits):
    parts = [((number >> bit) & 1) << (bits - 1 - bit) for bit in range(bits)]
    return functools.reduce(jnp.bitwise_or, parts)


def iota(shape, dim):
    return lax.broadcasted_iota(jnp.int32, shape, dim)


def grouping(shape, row_dim):
    out, column = iota(shape, row_dim), iota(shape, 1 - row_dim)

    def choose(level2, x1, x2, x3, far):
        return jnp.where(
            column < 16, level2,
            jnp.where(column < 48, x1, jnp.where(column < 64, x2, jnp.where(column < 80, x3, far))),
        )

    place = column - choose(0, 16, 48, 64, 80)
    row = jnp.where(column < 80, place & 3, reverse((place & 7) >> 1, 2))
    across = choose(0, 1, 2, 3, place >> 3)
    half = jnp.where(column < 80, 0, 1)
    weight = choose(0.25, 0.125, 0.25, 0.25, 0.5)
    return jnp.where(out == row * 8 + half * 4 + across, weight, 0.0).astype(BF16)


def two_heads(block):
    first = lax.broadcasted_iota(jnp.int32, block.shape, 1) < 64
    zero = jnp.zeros_like(block)
    return jnp.concatenate([jnp.where(first, block, zero), jnp.where(first, zero, block)], axis=0)


def dot(left, right, dims=(((1,), (0,)), ((), ()))):
    return lax.dot_general(left, right, dims, preferred_element_type=F32)


def pool_kernel(keys_ref, values_ref, zero_ref, one_ref, two_ref, three_ref, keys, values, sems):
    moves = [
        pltpu.make_async_copy(source, target, sems.at[place])
        for place, (source, target) in enumerate(((keys_ref, keys), (values_ref, values)))
    ]
    for move in moves:
        move.start()
    place, token = iota((128, TOK), 0), iota((128, TOK), 1)

    def choose(zero, one, two, three):
        return jnp.where(
            place < 64, zero, jnp.where(place < 96, one, jnp.where(place < 112, two, three))
        )

    row = choose(reverse(place, 6), reverse(place, 5), reverse(place, 4), place - 112)
    weight = choose(1 / 4, 1 / 8, 1 / 16, 1 / 32)
    table = jnp.where((token >> choose(2, 3, 4, 5)) == row, weight, 0.0).astype(BF16)
    for half, (move, ref) in enumerate(zip(moves, (keys, values))):
        move.wait()
        pooled = dot(table, ref[...]).astype(BF16)
        columns = slice(half * D, (half + 1) * D)
        zero_ref[:, columns] = pooled[:64]
        one_ref[:, columns] = pooled[64:96]
        two_ref[:, columns] = pooled[96:112]
        three_ref[:, columns] = pooled[112:120]


def doubled(rows):
    half = 0.5 * rows
    return jnp.concatenate([half, half], axis=0)


def near_kernel(z3_ref, z2_ref, z1_ref, after_ref, out_ref):
    out_ref[:32] = z1_ref[...]
    out_ref[32:64] = z2_ref[...]
    out_ref[64:] = z3_ref[...]


def level6_kernel(level5_ref, y3_ref, y2_ref, y1_ref, low_x_ref, low_ref, level6_ref):
    low_ref[:96] = low_x_ref[...]
    low_ref[96:128] = y1_ref[...]
    low_ref[128:144] = y2_ref[...]
    low_ref[144:] = y3_ref[...]
    level6_ref[:8] = pair_mean(level5_ref[...])
    level6_ref[8:16] = pair_mean(pair_mean(y1_ref[...]))
    level6_ref[16:24] = pair_mean(y2_ref[...])
    level6_ref[24:] = pair_mean(y3_ref[...])


def pair_mean(rows):
    half = rows.shape[0] // 2
    return (0.5 * (rows[:half].astype(F32) + rows[half:].astype(F32))).astype(BF16)


def group_kernel(two_ref, far_ref, x3_ref, x2_ref, x1_ref, level4_ref, level5_ref, low_ref):
    low_ref[:32] = x1_ref[:32]
    low_ref[32:48] = x2_ref[:16]
    low_ref[48:64] = x3_ref[:16]
    low_ref[64:72] = far_ref[...]
    low_ref[72:80] = x1_ref[32:]
    low_ref[80:88] = x2_ref[16:]
    low_ref[88:] = x3_ref[16:]
    level4 = dot(grouping((32, 112), 0), jnp.concatenate([two_ref[...], low_ref[...]], axis=0)).astype(BF16)
    level4_ref[...] = level4
    level5_ref[...] = (0.5 * (level4[:16].astype(F32) + level4[16:].astype(F32))).astype(BF16)


def y_send_kernel(b3_ref, b2_ref, b1_ref, own_ref, other_ref, y1_ref, y2_ref, y3_ref, g6_ref):
    shared = 0.5 * (b2_ref[...].astype(F32) + b3_ref[...].astype(F32))
    for core, y_ref in enumerate((own_ref, other_ref)):
        wide_rows, rows = slice(core * 32, core * 32 + 32), slice(core * 16, core * 16 + 16)
        g6 = b1_ref[wide_rows].astype(F32) + shared
        g6_ref[wide_rows] = g6
        y1_ref[wide_rows] = (y_ref[:32] + doubled(doubled(g6[8:16]))).astype(BF16)
        y2_ref[rows] = (y_ref[32:48] + doubled(g6[16:24])).astype(BF16)
        y3_ref[rows] = (y_ref[48:] + doubled(g6[24:])).astype(BF16)


def x_send_kernel(b3_ref, b2_ref, b1_ref, g6_ref, own_ref, other_ref, x1_ref, x2_ref, x3_ref, two_ref, far_ref
):
    table = grouping((112, 32), 1)
    for core, x_ref in enumerate((own_ref, other_ref)):
        wide_rows, rows = slice(core * 32, core * 32 + 32), slice(core * 16, core * 16 + 16)
        g5 = doubled(g6_ref[core * 32 : core * 32 + 8])
        g5 = g5 + b2_ref[rows].astype(F32) + b3_ref[rows].astype(F32)
        g = dot(table, (b1_ref[wide_rows].astype(F32) + doubled(g5)).astype(BF16))
        two_ref[rows] = g[:16]
        x = x_ref[...] + g[16:]
        far = slice(core * 8, core * 8 + 8)
        x1_ref[wide_rows] = x[:32].astype(BF16)
        x1_ref[64 + core * 8 : 72 + core * 8] = x[72:80].astype(BF16)
        for ref, first, second in ((x2_ref, 32, 80), (x3_ref, 48, 88)):
            ref[rows] = x[first : first + 16].astype(BF16)
            ref[32 + core * 8 : 40 + core * 8] = x[second : second + 8].astype(BF16)
        far_ref[far] = x[64:72]


def core_send_kernel(b3_ref, b2_ref, b1_ref, two_ref, far_ref, zero_ref, out_ref, one_ref, own_far_ref):
    for core in range(2):
        wide_rows, rows = slice(core * 32, core * 32 + 32), slice(core * 16, core * 16 + 16)
        near, far = slice(core * 8, core * 8 + 8), slice(32 + core * 8, 40 + core * 8)
        two = two_ref[rows] + b2_ref[rows].astype(F32) + b3_ref[rows].astype(F32)
        one = doubled(b1_ref[wide_rows].astype(F32) + doubled(two))
        last = b2_ref[far].astype(F32) + b3_ref[far].astype(F32)
        last = last + far_ref[near] + b1_ref[64 + core * 8 : 72 + core * 8].astype(F32)
        if core == 0:
            one_ref[...] = one
            own_far_ref[...] = last
        else:
            out_ref[:64] = (zero_ref[...] + one).astype(BF16)
            out_ref[64:] = last.astype(BF16)


def of_pair(ref, pair, rows=slice(None), shift=0):
    return ref[rows, shift + pair * LANES : shift + (pair + 1) * LANES]


def of_block(refs, pair, rows):
    return of_pair(refs[0], pair, rows), of_pair(refs[-1], pair, rows, 2 * D // len(refs) - D)


def of_blocks(blocks, pair, rows):
    parts = [of_block(block, pair, part) for block, part in zip(blocks, rows)]
    return [jnp.concatenate(side, axis=0) for side in zip(*parts)]


def store_pair(ref, pair, gk, gv):
    ref[:, pair * LANES : (pair + 1) * LANES] = gk.astype(ref.dtype)
    ref[:, D + pair * LANES : D + (pair + 1) * LANES] = gv.astype(ref.dtype)


def take(refs, counts):
    refs = iter(refs)
    return [[next(refs) for unused in range(count)] for count in counts]


def stats_kernel(counts, q_ref, do_ref, *refs):
    out_ref = refs[-1]
    blocks = take(refs, counts)
    for pair in range(PAIRS):
        q2 = two_heads(of_pair(q_ref, pair) * SCALE)
        d2 = two_heads(of_pair(do_ref, pair))
        k, v = of_blocks(blocks, pair, [slice(None)] * len(blocks))
        scores = dot(k, q2, NT)
        largest = jnp.max(scores, axis=0, keepdims=True)
        expsc = jnp.exp(scores - largest)
        out_ref[pair, 0:1] = largest
        out_ref[pair, 1:2] = jnp.sum(expsc, axis=0, keepdims=True)
        out_ref[pair, 2:3] = jnp.sum(expsc * dot(v, d2, NT), axis=0, keepdims=True)


def top_kernel(q_ref, do_ref, top_ref, low_ref, z1_ref, z2_ref, z3_ref, out_ref):
    for pair in range(PAIRS):
        q2 = two_heads(of_pair(q_ref, pair) * SCALE)
        d2 = two_heads(of_pair(do_ref, pair))
        k, v = of_block([top_ref], pair, slice(None))
        scores = dot(k, q2, NT)
        dprobs = dot(v, d2, NT)
        low_largest = low_ref[pair, 0:1]
        largest = jnp.maximum(jnp.max(scores, axis=0, keepdims=True), low_largest)
        expsc = jnp.exp(scores - largest)
        low_part = jnp.exp(low_largest - largest)
        total = jnp.sum(expsc, axis=0, keepdims=True) + low_ref[pair, 1:2] * low_part
        inner = jnp.sum(expsc * dprobs, axis=0, keepdims=True) + low_ref[pair, 2:3] * low_part
        share = 1.0 / total
        inner = inner * share
        out_ref[pair, 0:1] = largest
        out_ref[pair, 1:2] = share
        out_ref[pair, 2:3] = inner
        probs = expsc * share
        dscores = (probs * (dprobs - inner)).astype(BF16)
        gk, gv = dot(dscores, q2), dot(probs.astype(BF16), d2)
        store_pair(z1_ref, pair, gk[:64], gv[:64])
        store_pair(z2_ref, pair, gk[64:96], gv[64:96])
        store_pair(z3_ref, pair, gk[96:], gv[96:])


def grads_kernel(counts, rows, first, last, q_ref, do_ref, stats_ref, *refs):
    blocks = take(refs, counts)
    rest = list(refs[sum(counts) :])
    before = [] if first else [rest.pop(0), rest.pop(0)]
    rest.pop(0)
    mixed_ref, gq_ref = rest.pop(0), rest.pop(0)
    g_refs = rest
    for pair in range(PAIRS):
        q2 = two_heads(of_pair(q_ref, pair) * SCALE)
        d2 = two_heads(of_pair(do_ref, pair))
        k, v = of_blocks(blocks, pair, rows)
        probs = jnp.exp(dot(k, q2, NT) - stats_ref[pair, 0:1]) * stats_ref[pair, 1:2]
        dscores = (probs * (dot(v, d2, NT) - stats_ref[pair, 2:3])).astype(BF16)
        weights = probs.astype(BF16)
        mixed, gq = dot(v, weights, TN), dot(k, dscores, TN)
        count = sum(ref.shape[0] for ref in g_refs)
        gk, gv, start = dot(dscores[:count], q2), dot(weights[:count], d2), 0
        for ref in g_refs:
            store_pair(ref, pair, gk[start : start + ref.shape[0]], gv[start : start + ref.shape[0]])
            start += ref.shape[0]

        def pick(both):
            return jnp.concatenate([both[:64, :TOK], both[64:, TOK:]], axis=0)

        mixed, gq = pick(mixed), pick(gq)
        if before:
            mixed, gq = mixed + before[0][pair], gq + before[1][pair]
        if last:
            columns = slice(pair * LANES, (pair + 1) * LANES)
            mixed_ref[:, columns] = mixed.T.astype(BF16)
            gq_ref[:, columns] = (gq * SCALE).T.astype(BF16)
        else:
            mixed_ref[pair] = mixed
            gq_ref[pair] = gq


def finish_kernel(first_ref, second_ref, zero_ref, out_ref):
    place = reverse(iota((TOK, 64), 1), 6)
    unpooling = jnp.where((iota((TOK, 64), 0) >> 2) == place, 0.25, 0.0).astype(BF16)
    high = zero_ref[...].astype(BF16)
    low = (zero_ref[...] - high.astype(F32)).astype(BF16)
    for half, ref in enumerate((first_ref, second_ref)):
        rows = slice(half * TOK // 2, (half + 1) * TOK // 2)
        table = unpooling[rows]
        out_ref[rows] = ref[...] + dot(table, high) + dot(table, low)


def last_kernel(near_ref, part_ref, keys_ref, values_ref):
    part = part_ref[...].astype(F32) * (8 / TOK)
    for group in range(8):
        rows = slice(group * (TOK // 8), (group + 1) * (TOK // 8))
        total = (near_ref[rows] + part[group : group + 1]).astype(BF16)
        keys_ref[rows] = total[:, :D]
        values_ref[rows] = total[:, D:]


POOL_VMEM = 536 * 2**20 // 10
STATS = jax.ShapeDtypeStruct((PAIRS, 8, 2 * TOK), F32)
PARTIAL = jax.ShapeDtypeStruct((PAIRS, LANES, TOK), F32)


def call(kernel, operands, out_shape, flops, name, ordered=False):
    in_specs = [pl.BlockSpec(memory_space=pltpu.VMEM)] * len(operands)
    if ordered:
        in_specs[-1] = pl.BlockSpec(memory_space=pl.ANY)
    return pl.pallas_call(
        kernel,
        in_specs=in_specs,
        out_shape=out_shape,
        compiler_params=pltpu.CompilerParams(vmem_limit_bytes=40 * 2**20),
        cost_estimate=pl.CostEstimate(flops=flops, bytes_accessed=2**20, transcendentals=0),
        name=name,
    )(*operands)


def matmul_cost(keys, count):
    return 2 * count * keys * 2 * TOK * LANES * PAIRS


def low_stats(queries, cotangent, blocks):
    return call(
        functools.partial(stats_kernel, [len(block) for block in blocks]),
        [queries, cotangent] + [array for block in blocks for array in block],
        STATS, matmul_cost(5 * LANES, 2), "low_stats",
    )


def top_part(queries, cotangent, top, low):
    rows = top.shape[0]
    return call(
        top_kernel, [queries, cotangent, top, low], [wide(64), wide(32), wide(32), STATS],
        matmul_cost(rows, 4), "top_part",
    )


def grads_part(queries, cotangent, stats, blocks, wanted, before, after, last, name):
    operands = [queries, cotangent, stats]
    out_shape = [jax.ShapeDtypeStruct((TOK, D), BF16)] * 2 if last else [PARTIAL] * 2
    counts, rows, total = [], [], 0
    for (arrays, start, size), want in zip(blocks, wanted):
        operands += arrays
        counts.append(len(arrays))
        rows.append(slice(start, start + size))
        total += size
        if want:
            out_shape = out_shape + [jax.ShapeDtypeStruct((size, 2 * D), want)]
    return call(
        functools.partial(grads_kernel, counts, rows, not before, last),
        operands + [*before, after], out_shape, matmul_cost(total, 6), name, True,
    )


def wide(rows):
    return jax.ShapeDtypeStruct((rows, 2 * D), BF16)


def wide_f32(rows):
    return jax.ShapeDtypeStruct((rows, 2 * D), F32)


def pool(keys, values):
    return pl.pallas_call(
        pool_kernel,
        in_specs=[pl.BlockSpec(memory_space=pl.ANY)] * 2,
        out_specs=[pl.BlockSpec(memory_space=pltpu.VMEM)] * 4,
        out_shape=[wide(64), wide(32), wide(16), wide(8)],
        scratch_shapes=[
            pltpu.VMEM((TOK, D), BF16),
            pltpu.VMEM((TOK, D), BF16),
            pltpu.SemaphoreType.DMA((2,)),
        ],
        compiler_params=pltpu.CompilerParams(vmem_limit_bytes=POOL_VMEM),
        name="pool",
    )(keys, values)


def whole(kernel, out_shape, name, ordered=None):
    extra = {} if ordered is None else {
        "in_specs": [pl.BlockSpec(memory_space=pltpu.VMEM)] * ordered + [pl.BlockSpec(memory_space=pl.ANY)]
    }
    return pl.pallas_call(
        kernel,
        out_shape=out_shape,
        compiler_params=pltpu.CompilerParams(vmem_limit_bytes=16 * 2**20),
        name=name,
        **extra,
    )


def mean(one, two):
    return (0.5 * (one.astype(F32) + two.astype(F32))).astype(BF16)


def joined(*blocks):
    return jnp.concatenate(blocks, axis=0)


def other_core(value):
    return flip(value, "lo", 1)


def shards(queries, keys, values, cotangent):
    zero, one, two, three = pool(keys, values)
    far = flip(three, "lo", 8)
    sec0 = other_core(zero)
    short = joined(two, far)
    x1 = flip(joined(one, far), "lo", 2)
    x2 = flip(short, "lo", 4)
    x3 = flip(short, "lo", 6)
    level4, level5, low_x = whole(group_kernel, [wide(32), wide(16), wide(96)], "group")(
        two, far, x3, x2, x1
    )
    y1 = flip(level4, "hi", 1)
    y2 = flip(level5, "hi", 2)
    y3 = flip(level5, "hi", 3)
    low, level6 = whole(level6_kernel, [wide(160), wide(32)], "level6")(level5, y3, y2, y1, low_x)
    z1 = flip(level6, "hi", 4)
    z2 = flip(level6, "hi", 8)
    z3 = flip(level6, "hi", 12)
    low2 = other_core(low)
    low_stat = low_stats(
        queries, cotangent,
        [(keys, values)] + [(rows,) for rows in (sec0, low, low2)],
    )
    near = whole(near_kernel, wide(96), "near", 3)(z3, z2, z1, low_stat)
    mate = other_core(near)
    top = joined(near[:32], mate[:32], mean(near[32:], mate[32:]))

    z1, z2, z3, stats = top_part(queries, cotangent, top, low_stat)
    b1 = flip(z1, "hi", 4)
    b2 = flip(z2, "hi", 8)
    b3 = flip(z3, "hi", 12)
    mixed, gq, y_g, y_other = grads_part(
        queries, cotangent, stats, [([low], 96, 64), ([low2], 96, 64), ([top], 0, 128)],
        (F32, F32, None), [], z1, False, "y_grads",
    )
    y1, y2, y3, g6 = whole(y_send_kernel, [wide(64), wide(32), wide(32), wide_f32(64)], "y_send")(
        b3, b2, b1, y_g, y_other
    )
    b1 = flip(y1, "hi", 1)
    b2 = flip(y2, "hi", 2)
    b3 = flip(y3, "hi", 3)
    mixed, gq, x_g, x_other, first_g = grads_part(
        queries, cotangent, stats,
        [([low], 0, 96), ([low2], 0, 96), ([keys, values], 0, TOK // 2)],
        (F32,) * 3, [mixed, gq], y1, False, "x_grads",
    )
    x1, x2, x3, two_g, far_g = whole(
        x_send_kernel, [wide(80), wide(48), wide(48), wide_f32(32), wide_f32(16)], "x_send"
    )(b3, b2, b1, g6, x_g, x_other)
    b1 = flip(x1, "lo", 2)
    b2 = flip(x2, "lo", 4)
    b3 = flip(x3, "lo", 6)
    mixed, grad_queries, sec0_g, second_g = grads_part(
        queries, cotangent, stats, [([sec0], 0, 64), ([keys, values], TOK // 2, TOK // 2)],
        (F32,) * 2, [mixed, gq], x1, True, "own_grads",
    )
    mate_g, one_g, far_g = whole(core_send_kernel, [wide(72), wide_f32(64), wide_f32(8)], "core_send")(
        b3, b2, b1, two_g, far_g, sec0_g
    )
    back = other_core(mate_g).astype(F32)
    last = flip((far_g + back[64:]).astype(BF16), "lo", 8)
    near = whole(finish_kernel, jax.ShapeDtypeStruct((TOK, 2 * D), F32), "finish")(
        first_g, second_g, back[:64] + one_g
    )
    grad_keys, grad_values = whole(
        last_kernel, [jax.ShapeDtypeStruct((TOK, D), BF16)] * 2, "add_last"
    )(near, last)
    return (mixed, grad_queries, grad_keys, grad_values)


def solution(mesh):
    spec = P(("hi", "lo"), None)
    return jax.shard_map(
        shards, mesh=mesh, in_specs=(spec,) * 4, out_specs=(spec,) * 4, check_vma=False
    )
```
